128 devices in a mesh: gx: 16 (over y, z), gy: 8 (over x, core).
Axes of the slice: x: 4, y: 4, z: 4, core: 2. Of those that a mesh axis runs over, the one named last changes fastest.
Arguments:
- token_query: bfloat16 [163840, 512], P(('gx', 'gy')), may hold values from -6 to 6
- token_key: bfloat16 [163840, 512], P(('gx', 'gy')), may hold values from -6 to 6
- token_value: bfloat16 [163840, 512], P(('gx', 'gy')), may hold values from -6 to 6
- cotangent: bfloat16 [163840, 512], P(('gx', 'gy')), may hold values from -16 to 16
- anchor_keys: bfloat16 [64, 512], replicated, may hold values from -6.5 to 6.5
- anchor_values: bfloat16 [64, 512], replicated, may hold values from -6 to 6
- partner: int32 [1280, 2], P(('gx', 'gy')), may hold values from 0 to 1279, as said below
- cluster: int32 [1280, 10], P(('gx', 'gy')), may hold values from 0 to 9, each once within a row
- lengths: int32 [1280], P(('gx', 'gy')), may hold values from 1 to 10, as said below
Outputs:
- query_grad: bfloat16 [163840, 512], P(('gx', 'gy'))
- key_grad: bfloat16 [163840, 512], P(('gx', 'gy'))
- value_grad: bfloat16 [163840, 512], P(('gx', 'gy'))
- anchor_grads: float32 [2, 64, 512], replicated
The draws below stay inside these ranges and needn't reach their ends.
Inputs may be any that keep to these rules, and one draw needn't show every extreme that they name: Expander partners: for each map m, partner[partner[b, m], m] == b; a partner lies on a device with the same gy index and another gx index. Of one device's blocks, at most 2 entries name blocks of any one other device, and exactly 2 for some pairs of devices in every draw. A partner's position within its device and the XOR of its gx index with the block's gx index depend only on the block's position, the map and the gy index. `cluster`: each row is a permutation of the positions of the blocks held by the query block's own device; entries from lengths[b] on are not used. `lengths`: some block has exactly 10.
All inputs are finite; a program needn't handle non-finite values.
Results may differ from the reference program's by a relative error of at most 0.0084.
Values may be sent and summed in bfloat16 or wider, within the bound.
No kernel may reach another device: no remote copies, remote signals or barrier semaphores. Data moves between devices by JAX's collectives and lax.ppermute only.
A program may use at most 192 MiB of HBM per device.

```python
import jax
import jax.numpy as jnp
from jax import lax

HEADS = 8
HEAD_DIM = 64
D = 512
BLK = 128
GLOBAL = 64
EXPN = 2
BLK_DEV = 10
NBLK = 1280
TOKENS = 163840
N_GX = 16
N_GY = 8


def draw_token_query(key, part):
    key = jax.random.fold_in(key, 11)
    first_key = jax.random.fold_in(key, 0)
    full_shape = (TOKENS, HEADS * HEAD_DIM)
    result = jax.random.truncated_normal(first_key, -6.0, 6.0, full_shape, jnp.float32)
    return result.astype(jnp.bfloat16)


def draw_anchor_keys(key, part):
    key = jax.random.fold_in(key, 12)
    full_shape = (GLOBAL, HEADS * HEAD_DIM)
    result = jax.random.truncated_normal(key, -6.0, 6.0, full_shape, jnp.float32)
    return result.astype(jnp.bfloat16)


def draw_partner(key, part):
    key = jax.random.fold_in(key, 13)
    half_block = BLK_DEV // 2
    pair_count = EXPN * half_block

    def row_pattern(row_key):
        row_keys = jax.random.split(row_key, EXPN + 2)
        pair_order = jax.random.permutation(row_keys[0], pair_count)
        pair_shift = jax.random.randint(row_keys[1], (), 0, N_GX - 1)
        offset = (1 + (pair_order + pair_shift) % (N_GX - 1)).astype(jnp.int32)
        mate_list = []
        flip_list = []
        for which_map in range(EXPN):
            shuffled = jax.random.permutation(row_keys[2 + which_map], BLK_DEV).astype(jnp.int32)
            left_side = shuffled[0::2]
            right_side = shuffled[1::2]
            mate_now = jnp.zeros((BLK_DEV,), jnp.int32).at[left_side].set(right_side).at[right_side].set(left_side)
            flip_pairs = offset[which_map * half_block:(which_map + 1) * half_block]
            flip_now = jnp.zeros((BLK_DEV,), jnp.int32).at[left_side].set(flip_pairs).at[right_side].set(flip_pairs)
            mate_list.append(mate_now)
            flip_list.append(flip_now)
        return (jnp.stack(mate_list, 1), jnp.stack(flip_list, 1))
    mate_all, flip_all = jax.vmap(row_pattern)(jax.random.split(key, N_GY))
    column = jnp.arange(N_GX, dtype=jnp.int32)[:, None, None, None]
    row_index = jnp.arange(N_GY, dtype=jnp.int32)[None, :, None, None]
    target = jnp.bitwise_xor(column, flip_all[None])
    block_ids = (target * N_GY + row_index) * BLK_DEV + mate_all[None]
    return block_ids.reshape(NBLK, EXPN).astype(jnp.int32)


def draw_lengths(key, part):
    key = jax.random.fold_in(key, 14)
    level_key, busy_key, length_key = jax.random.split(key, 3)
    device_count = NBLK // BLK_DEV
    spread = jax.random.randint(level_key, (device_count,), 0, BLK_DEV)
    levels = 1 + spread * spread * spread // (BLK_DEV * BLK_DEV)
    busiest = jax.random.randint(busy_key, (), 0, device_count)
    levels = jnp.where(jnp.arange(device_count) == busiest, BLK_DEV, levels)
    raw_lengths = jax.random.randint(length_key, (device_count, BLK_DEV), 0, 1 << 20) % levels[:, None] + 1
    raw_lengths = raw_lengths.at[busiest, 0].set(BLK_DEV)
    return raw_lengths.reshape(NBLK).astype(jnp.int32)


def shard_levels(rng, dims, cuts, least, top_value):
    level = 1.0
    for axis_at, parts in cuts:
        heights = jax.random.uniform(jax.random.fold_in(jax.random.fold_in(rng, 6), axis_at), (parts,), jnp.float32, least / len(cuts), top_value / len(cuts))
        level = level * jnp.repeat(jnp.exp(heights), dims[axis_at] // parts).reshape((-1,) + (1,) * (len(dims) - 1 - axis_at))
    return level


def scatter_about(key, dims, scale, reach, shards=(), held_as=jnp.bfloat16):
    gain = shard_levels(key, dims, shards, -0.22, 0.18) if shards else 1.0
    array = jax.random.normal(key, dims, jnp.float32) * scale * gain
    return jnp.minimum(jnp.maximum(array, -reach), reach).astype(held_as)


def setup_inputs(seed: int = 0) -> dict:
    arg_keys = jax.random.split(jax.random.key(seed), 10)
    token_query = draw_token_query(jax.random.fold_in(arg_keys[9], 71), 0)
    token_key = scatter_about(arg_keys[1], (TOKENS, D), 1.0, 6.0, ((0, 128),))
    token_value = scatter_about(arg_keys[2], (TOKENS, D), 1.0, 6.0, ((0, 128),))
    cotangent = scatter_about(arg_keys[3], (TOKENS, D), 4.0, 16.0, ((0, 128),))
    anchor_keys = draw_anchor_keys(jax.random.fold_in(arg_keys[9], 71), 0)
    anchor_values = scatter_about(arg_keys[5], (GLOBAL, D), 1.0, 6.0)
    partner = draw_partner(jax.random.fold_in(arg_keys[9], 71), 0)
    cluster = jax.vmap(lambda own: jax.random.permutation(own, BLK_DEV))(jax.random.split(arg_keys[7], NBLK)).reshape((NBLK, BLK_DEV)).astype(jnp.int32)
    lengths = draw_lengths(jax.random.fold_in(arg_keys[9], 71), 0)
    return {"token_query": token_query, "token_key": token_key, "token_value": token_value, "cotangent": cotangent, "anchor_keys": anchor_keys, "anchor_values": anchor_values, "partner": partner, "cluster": cluster, "lengths": lengths}


def reference(token_query, token_key, token_value, cotangent, anchor_keys, anchor_values, partner, cluster, lengths):
    features = HEADS * HEAD_DIM
    score_scale = HEAD_DIM ** -0.5
    listed = BLK_DEV + EXPN
    query_blocks = token_query.reshape(NBLK, BLK, features)
    key_blocks = token_key.reshape(NBLK, BLK, features)
    value_blocks = token_value.reshape(NBLK, BLK, features)
    cotan_blocks = cotangent.reshape(NBLK, BLK, features)

    def block_step(totals, block_index):
        key_acc, value_acc, key_anchor, value_anchor = totals
        device_base = (block_index // BLK_DEV) * BLK_DEV
        block_ids = jnp.concatenate([device_base + cluster[block_index], partner[block_index]]).astype(jnp.int32)
        keys_all = jnp.concatenate([key_blocks[block_ids].reshape(-1, features), anchor_keys], 0).astype(jnp.float32)
        values_all = jnp.concatenate([value_blocks[block_ids].reshape(-1, features), anchor_values], 0).astype(jnp.float32)
        keys_split = keys_all.reshape(-1, HEADS, HEAD_DIM)
        values_split = values_all.reshape(-1, HEADS, HEAD_DIM)
        queries = query_blocks[block_index].astype(jnp.float32).reshape(BLK, HEADS, HEAD_DIM)
        cotan_rows = cotan_blocks[block_index].astype(jnp.float32).reshape(BLK, HEADS, HEAD_DIM)
        column = jnp.arange(listed * BLK + GLOBAL, dtype=jnp.int32)
        live_mask = (column < lengths[block_index] * BLK) | (column >= BLK_DEV * BLK)
        scores = jnp.einsum("qhd,khd->hqk", queries, keys_split) * score_scale
        scores = jnp.where(live_mask, scores, -jnp.inf)
        dprobs = jnp.einsum("qhd,khd->hqk", cotan_rows, values_split)
        highest = jnp.max(scores, axis=-1, keepdims=True)
        log_total = highest + jnp.log(jnp.sum(jnp.exp(scores - highest), axis=-1, keepdims=True))
        weights = jnp.exp(scores - log_total)
        row_delta = jnp.sum(weights * dprobs, axis=-1, keepdims=True)
        dscore = lax.optimization_barrier((weights * (dprobs - row_delta) * score_scale).astype(jnp.bfloat16)).astype(jnp.float32)
        low_weights = lax.optimization_barrier(weights.astype(jnp.bfloat16)).astype(jnp.float32)
        query_out = jnp.einsum("hqk,khd->qhd", dscore, keys_split).reshape(BLK, features).astype(jnp.bfloat16)
        key_part = jnp.einsum("hqk,qhd->khd", dscore, queries).reshape(-1, features)
        value_part = jnp.einsum("hqk,qhd->khd", low_weights, cotan_rows).reshape(-1, features)
        key_acc = key_acc.at[block_ids].add(key_part[:listed * BLK].reshape(listed, BLK, features))
        value_acc = value_acc.at[block_ids].add(value_part[:listed * BLK].reshape(listed, BLK, features))
        key_anchor = key_anchor + key_part[listed * BLK:]
        value_anchor = value_anchor + value_part[listed * BLK:]
        return (key_acc, value_acc, key_anchor, value_anchor), query_out

    zero_blocks = jnp.zeros((NBLK, BLK, features), jnp.float32)
    zero_anchor = jnp.zeros((GLOBAL, features), jnp.float32)
    start_state = (zero_blocks, zero_blocks, zero_anchor, zero_anchor)
    totals, query_out = lax.scan(block_step, start_state, jnp.arange(NBLK, dtype=jnp.int32))
    key_acc, value_acc, key_anchor, value_anchor = totals
    return (query_out.reshape(TOKENS, features),
            key_acc.reshape(TOKENS, features).astype(jnp.bfloat16),
            value_acc.reshape(TOKENS, features).astype(jnp.bfloat16),
            jnp.stack([key_anchor, value_anchor]))
```

```python
import functools

import jax
import jax.numpy as jnp
from jax import lax
from jax.experimental import pallas as pl
from jax.experimental.pallas import tpu as pltpu
from jax.sharding import PartitionSpec as P

HEADS = 8
HEAD_DIM = 64
PAIRS = HEADS // 2
LANES = 2 * HEAD_DIM
SCALE = HEAD_DIM ** (-0.5)
LOG2E = 1.4426950408889634
EXP_SCALE = SCALE * LOG2E
CHUNK = 2
F32 = jnp.float32
BF16 = jnp.bfloat16


def pair_lanes(pair):
    return slice(pair * LANES, (pair + 1) * LANES)


def dot_nt(left, right):
    return lax.dot_general(left, right, (((1,), (1,)), ((), ())), preferred_element_type=F32)


def dot_nn(left, right):
    return jnp.dot(left, right, preferred_element_type=F32)


def dot_tn(left, right):
    return lax.dot_general(left, right, (((0,), (0,)), ((), ())), preferred_element_type=F32)


def head_masks():
    lane = lax.broadcasted_iota(jnp.int32, (1, LANES), 1)
    first = jnp.where(lane < HEAD_DIM, 1.0, 0.0)
    return first.astype(BF16), (1.0 - first).astype(BF16)


def pair_rows(rows_in, masks):
    return jnp.concatenate([rows_in * masks[0], rows_in * masks[1]], axis=0)


def stat_row(stats, pair, offset):
    at = offset + 2 * pair
    return jnp.concatenate([stats[at : at + 1], stats[at + 1 : at + 2]], axis=1)


def store_stats(stat_ref, slot, pair, log_total, delta):
    rows = log_total.shape[1] // 2
    for at, row in ((2 * pair, log_total), (HEADS + 2 * pair, delta)):
        stat_ref[slot, at : at + 1, :] = row[:, :rows]
        stat_ref[slot, at + 1 : at + 2, :] = row[:, rows:]


def first_sums(scores, dprobs):
    highest = jnp.max(scores, axis=0, keepdims=True) * EXP_SCALE
    terms = jnp.exp2(scores * EXP_SCALE - highest)
    return highest, jnp.sum(terms, axis=0, keepdims=True), jnp.sum(terms * dprobs, axis=0, keepdims=True)


def more_sums(state, scores, dprobs):
    highest, total, mass = state
    new_highest = jnp.maximum(highest, jnp.max(scores, axis=0, keepdims=True) * EXP_SCALE)
    shrink = jnp.exp2(highest - new_highest)
    terms = jnp.exp2(scores * EXP_SCALE - new_highest)
    return (
        new_highest,
        total * shrink + jnp.sum(terms, axis=0, keepdims=True),
        mass * shrink + jnp.sum(terms * dprobs, axis=0, keepdims=True),
    )


def finish_sums(state):
    highest, total, mass = state
    return highest + jnp.log(total) * LOG2E, mass / total


def weights_of(scores, dprobs, log_total, delta):
    weights = jnp.exp2(scores * EXP_SCALE - log_total)
    return weights.astype(BF16), (weights * (dprobs - delta)).astype(BF16)


def together(parts, axis):
    return parts[0] if len(parts) == 1 else jnp.concatenate(parts, axis=axis)


def staggered(items, begin, finish):
    ahead = None
    for item in items:
        begun = begin(item)
        if ahead is not None:
            finish(*ahead)
        ahead = (item, begun)
    finish(*ahead)


def block_rows_at(index, rows):
    return pl.ds(pl.multiple_of(index * rows, rows), rows)


def in_chunks(count, work, state):
    state = lax.fori_loop(0, count // CHUNK, lambda at, held: work(at * CHUNK, CHUNK, held), state)
    return lax.fori_loop(count // CHUNK * CHUNK, count, lambda at, held: work(at, 1, held), state)


def near_stats_kernel(
    cluster, lengths, slots, query_ref, cotan_ref, key_ref, value_ref, akey_ref, avalue_ref,
    stat_ref, keyt_ref, send_ref, qturn, oturn, sems,
):
    block = pl.program_id(0)
    block_count = pl.num_programs(0)
    rows, width = stat_ref.shape[2], query_ref.shape[1]
    fanout = slots.shape[0] // (query_ref.shape[0] // rows)

    def send_copies():
        for entry in range(slots.shape[0]):
            own = pl.ds(entry // fanout * rows, rows)
            slot = send_ref.at[slots[entry]]
            yield pltpu.make_async_copy(query_ref.at[own], slot.at[:, pl.ds(0, width)], sems.at[0, entry])
            yield pltpu.make_async_copy(cotan_ref.at[own], slot.at[:, pl.ds(width, width)], sems.at[1, entry])

    @pl.when(block == 0)
    def _():
        for copy in send_copies():
            copy.start()

    masks = head_masks()
    own = block_rows_at(block, rows)
    start = []
    for pair in range(PAIRS):
        lanes = pair_lanes(pair)
        qturn[pair] = pair_rows(query_ref[own, lanes], masks).T
        oturn[pair] = pair_rows(cotan_ref[own, lanes], masks).T
        keyt_ref[0, lanes, :] = key_ref[own, lanes].T
        start.append(
            first_sums(dot_nn(akey_ref[:, lanes], qturn[pair]), dot_nn(avalue_ref[:, lanes], oturn[pair]))
        )

    def work(first, count, states):
        spots = [
            block_rows_at(cluster[block * block_count + first + which], rows) for which in range(count)
        ]
        states = list(states)

        def begin(pair):
            lanes = pair_lanes(pair)
            return (
                dot_nn(together([key_ref[at, lanes] for at in spots], 0), qturn[pair]),
                dot_nn(together([value_ref[at, lanes] for at in spots], 0), oturn[pair]),
            )

        def finish(pair, tiles):
            states[pair] = more_sums(states[pair], *tiles)

        staggered(range(PAIRS), begin, finish)
        return tuple(states)

    states = in_chunks(lengths[block], work, tuple(start))
    for pair in range(PAIRS):
        store_stats(stat_ref, 0, pair, *finish_sums(states[pair]))

    @pl.when(block == block_count - 1)
    def _():
        for copy in send_copies():
            copy.wait()


def far_tiles(far_ref, keys, values, pair, masks):
    lanes = pair_lanes(pair)
    width = far_ref.shape[2] // 2
    queries = pair_rows(far_ref[0, :, lanes], masks)
    cotans = pair_rows(far_ref[0, :, width + lanes.start : width + lanes.stop], masks)
    return dot_nt(keys, queries), dot_nt(values, cotans), queries, cotans


def far_stats_kernel(slots, *refs, fanout):
    far_refs, (key_ref, value_ref, stat_ref) = refs[:fanout], refs[fanout:]
    masks = head_masks()
    step = pl.program_id(0)

    def begin(item):
        which, pair = item
        return far_tiles(far_refs[which], key_ref[:, pair_lanes(pair)], value_ref[:, pair_lanes(pair)], pair, masks)

    def finish(item, tiles):
        which, pair = item
        store_stats(stat_ref, slots[step * fanout + which], pair, *finish_sums(first_sums(*tiles[:2])))

    staggered([(which, pair) for which in range(fanout) for pair in range(PAIRS)], begin, finish)


def totals_kernel(
    slots, near_ref, far_ref, query_ref, cotan_ref, akey_ref, avalue_ref, total_ref, send_ref, key_acc, value_acc
):
    block = pl.program_id(0)
    block_count = pl.num_programs(0)
    fanout = slots.shape[0] // near_ref.shape[0]

    @pl.when(block == 0)
    def _():
        key_acc[...] = jnp.zeros_like(key_acc)
        value_acc[...] = jnp.zeros_like(value_acc)

    mine = [slots[block * fanout + which] for which in range(fanout)]
    parts = [near_ref[block]] + [far_ref[slot] for slot in mine]
    logs = [part[:HEADS] for part in parts]
    highest = functools.reduce(jnp.maximum, logs)
    shares = [jnp.exp2(log - highest) for log in logs]
    total = sum(shares)
    mass = sum(share * part[HEADS:] for share, part in zip(shares, parts))
    stats = jnp.concatenate([highest + jnp.log(total) * LOG2E, mass / total], axis=0)
    total_ref[0] = stats
    for slot in mine:
        send_ref[slot, : 2 * HEADS, :] = stats

    masks = head_masks()

    def begin(pair):
        lanes = pair_lanes(pair)
        qpair = pair_rows(query_ref[:, lanes], masks)
        opair = pair_rows(cotan_ref[:, lanes], masks)
        return dot_nt(akey_ref[:, lanes], qpair), dot_nt(avalue_ref[:, lanes], opair), qpair, opair

    def finish(pair, tiles):
        scores, dprobs, qpair, opair = tiles
        weights, dscore = weights_of(scores, dprobs, stat_row(stats, pair, 0), stat_row(stats, pair, HEADS))
        key_acc[:, pair_lanes(pair)] += dot_nn(dscore, qpair)
        value_acc[:, pair_lanes(pair)] += dot_nn(weights, opair)

    staggered(range(PAIRS), begin, finish)

    @pl.when(block == block_count - 1)
    def _():
        slot_count = send_ref.shape[0]
        piece = 2 * key_acc.shape[0] // slot_count
        for slot in range(slot_count):
            acc, factor = (key_acc, SCALE) if slot < slot_count // 2 else (value_acc, 1.0)
            first = slot % (slot_count // 2) * piece
            for pair in range(PAIRS):
                at = 2 * HEADS + pair * piece
                send_ref[slot, at : at + piece, :] = acc[first : first + piece, pair_lanes(pair)] * factor


def unpair_turned(both):
    rows = both.shape[1] // 2
    feature = lax.broadcasted_iota(jnp.int32, (LANES, rows), 0)
    return jnp.where(feature < HEAD_DIM, both[:, :rows], both[:, rows:]).T


def far_query_kernel(slots, *refs, fanout):
    far_refs, stat_refs, refs = refs[:fanout], refs[fanout : 2 * fanout], refs[2 * fanout :]
    key_ref, value_ref, keyt_ref, out_ref = refs
    masks = head_masks()
    step = pl.program_id(0)
    stats = [stat_ref[0] for stat_ref in stat_refs]

    def begin(item):
        which, pair = item
        return far_tiles(far_refs[which], key_ref[:, pair_lanes(pair)], value_ref[:, pair_lanes(pair)], pair, masks)

    def finish(item, tiles):
        which, pair = item
        logs, deltas = stat_row(stats[which], pair, 0), stat_row(stats[which], pair, HEADS)
        _, dscore = weights_of(*tiles[:2], logs, deltas)
        far_grad = unpair_turned(dot_nn(keyt_ref[0, pair_lanes(pair), :], dscore)) * SCALE
        out_ref[slots[step * fanout + which], :, pair_lanes(pair)] = far_grad.astype(BF16)

    staggered([(which, pair) for which in range(fanout) for pair in range(PAIRS)], begin, finish)


def grads_kernel(
    cluster, lengths, slots, query_ref, cotan_ref, key_ref, value_ref, keyt_ref, akey_ref, avalue_ref, total_ref,
    *refs, fanout,
):
    far_refs, stat_refs, refs = refs[:fanout], refs[fanout : 2 * fanout], refs[2 * fanout :]
    dquery_ref, dkey_ref, dvalue_ref, qpair, opair, qturn, oturn, dq_acc, dk_acc, dv_acc = refs
    block = pl.program_id(0)
    block_count = pl.num_programs(0)
    rows, width = query_ref.shape

    @pl.when(block == 0)
    def _():
        dk_acc[...] = jnp.zeros_like(dk_acc)
        dv_acc[...] = jnp.zeros_like(dv_acc)

    masks = head_masks()
    stats = total_ref[0]
    logs = [stat_row(stats, pair, 0) for pair in range(PAIRS)]
    deltas = [stat_row(stats, pair, HEADS) for pair in range(PAIRS)]
    for pair in range(PAIRS):
        lanes = pair_lanes(pair)
        qpair[pair] = pair_rows(query_ref[:, lanes], masks)
        opair[pair] = pair_rows(cotan_ref[:, lanes], masks)
        qturn[pair] = qpair[pair].T
        oturn[pair] = opair[pair].T
        akeys = akey_ref[:, lanes]
        scores = dot_nn(akeys, qturn[pair])
        dprobs = dot_nn(avalue_ref[:, lanes], oturn[pair])
        _, dscore = weights_of(scores, dprobs, logs[pair], deltas[pair])
        dq_acc[pair] = dot_tn(akeys, dscore)

    def work(first, count, carry):
        ids = [cluster[block * block_count + first + which] for which in range(count)]
        spots = [block_rows_at(index, rows) for index in ids]

        def begin(pair):
            lanes = pair_lanes(pair)
            return (
                dot_nn(together([key_ref[at, lanes] for at in spots], 0), qturn[pair]),
                dot_nn(together([value_ref[at, lanes] for at in spots], 0), oturn[pair]),
            )

        def finish(pair, tiles):
            lanes = pair_lanes(pair)
            weights, dscore = weights_of(*tiles, logs[pair], deltas[pair])
            key_part = dot_nn(dscore, qpair[pair])
            value_part = dot_nn(weights, opair[pair])
            for which, at in enumerate(spots):
                part = slice(which * rows, (which + 1) * rows)
                dk_acc[at, lanes] += key_part[part]
                dv_acc[at, lanes] += value_part[part]
            dq_acc[pair] += dot_nn(together([keyt_ref[index, lanes, :] for index in ids], 1), dscore)

        staggered(range(PAIRS), begin, finish)
        return carry

    in_chunks(lengths[block], work, 0)
    for pair in range(PAIRS):
        dquery_ref[:, pair_lanes(pair)] = unpair_turned(dq_acc[pair]) * SCALE

    own = block_rows_at(block, rows)
    far_stats = [stat_ref[0] for stat_ref in stat_refs]

    def begin_far(pair):
        keys, values = key_ref[own, pair_lanes(pair)], value_ref[own, pair_lanes(pair)]
        return [far_tiles(far_ref, keys, values, pair, masks) for far_ref in far_refs]

    def finish_far(pair, tiles):
        lanes = pair_lanes(pair)
        both = [
            weights_of(*tile[:2], stat_row(far_stat, pair, 0), stat_row(far_stat, pair, HEADS))
            for tile, far_stat in zip(tiles, far_stats)
        ]
        dscores, weights = [dscore for _, dscore in both], [weights for weights, _ in both]
        dk_acc[own, lanes] += dot_nn(together(dscores, 1), together([tile[2] for tile in tiles], 0))
        dv_acc[own, lanes] += dot_nn(together(weights, 1), together([tile[3] for tile in tiles], 0))

    staggered(range(PAIRS), begin_far, finish_far)

    @pl.when(block == block_count - 1)
    def _():
        dkey_ref[...] = (dk_acc[...] * SCALE).astype(BF16)
        dvalue_ref[...] = dv_acc[...].astype(BF16)


def add_kernel(slots, near_ref, back_ref, out_ref, landed, sems):
    entry_count = slots.shape[0]
    rows = landed.shape[1]
    fanout = entry_count // (near_ref.shape[0] // rows)
    copies = [
        pltpu.make_async_copy(back_ref.at[slots[entry]], landed.at[entry], sems.at[entry])
        for entry in range(entry_count)
    ]
    for copy in copies:
        copy.start()
    for block in range(entry_count // fanout):
        own = pl.ds(block * rows, rows)
        total = near_ref[own, :]
        for entry in range(block * fanout, (block + 1) * fanout):
            copies[entry].wait()
            total = total + landed[entry].astype(F32)
        out_ref[own, :] = total.astype(BF16)


def cost(flops, bytes_accessed, exps):
    return pl.CostEstimate(flops=int(flops), bytes_accessed=int(bytes_accessed), transcendentals=int(exps))


def shards(token_query, token_key, token_value, cotangent, anchor_keys, anchor_values, partner, cluster, lengths):
    block_count, fanout = partner.shape
    tokens, width = token_query.shape
    rows = tokens // block_count
    anchors = anchor_keys.shape[0]
    line_size = lax.axis_size("gx")
    row_size = lax.axis_size("gy")
    entry_count = block_count * fanout
    capacity = 2 * ((entry_count // 2 + line_size - 2) // (line_size - 1))
    slot_count = line_size * capacity
    params = pltpu.CompilerParams(vmem_limit_bytes=40 * 1024 * 1024)

    entries = jnp.arange(entry_count, dtype=jnp.int32)
    targets = partner.reshape(-1)
    peer_index = targets // block_count // row_size
    ordering = targets * fanout + entries % fanout
    same_peer = peer_index[:, None] == peer_index[None, :]
    recv_slot = peer_index * capacity + jnp.sum(same_peer & (entries[None, :] < entries[:, None]), axis=1)
    send_slot = peer_index * capacity + jnp.sum(same_peer & (ordering[None, :] < ordering[:, None]), axis=1)
    recv_slot = recv_slot.astype(jnp.int32)
    send_slot = send_slot.astype(jnp.int32)
    near_ids = cluster.reshape(-1)

    def exchange(rows_out):
        return lax.all_to_all(rows_out, "gx", split_axis=0, concat_axis=0, tiled=True)

    pair_flops = 2 * rows * rows * width
    whole = lambda *shape: pl.BlockSpec(shape, lambda step, *_: (0,) * len(shape))
    per_block = pl.BlockSpec((rows, width), lambda step, *_: (step, 0))
    block_stats = pl.BlockSpec((1, 2 * HEADS, rows), lambda step, *_: (step, 0, 0))
    turned_block = pl.BlockSpec((1, width, rows), lambda step, *_: (step, 0, 0))
    hbm = pl.BlockSpec(memory_space=pl.ANY)
    stats_type = jax.ShapeDtypeStruct((block_count, 2 * HEADS, rows), F32)
    slot_stats_type = jax.ShapeDtypeStruct((slot_count, 2 * HEADS, rows), F32)
    send_type = jax.ShapeDtypeStruct((slot_count, 4 * HEADS, rows), F32)
    pair_scratch = pltpu.VMEM((PAIRS, 2 * rows, LANES), BF16)
    turned_scratch = pltpu.VMEM((PAIRS, LANES, 2 * rows), BF16)

    def slot_specs(shape):
        def spec(which):
            return pl.BlockSpec(shape, lambda step, *scalars: (scalars[-1][step * fanout + which], 0, 0))

        return [spec(which) for which in range(fanout)]

    near_stats, turned_keys, send_rows = pl.pallas_call(
        near_stats_kernel,
        grid_spec=pltpu.PrefetchScalarGridSpec(
            num_scalar_prefetch=3,
            grid=(block_count,),
            in_specs=[
                whole(tokens, width),
                whole(tokens, width),
                whole(tokens, width),
                whole(tokens, width),
                whole(anchors, width),
                whole(anchors, width),
            ],
            out_specs=[block_stats, turned_block, hbm],
            scratch_shapes=[turned_scratch, turned_scratch, pltpu.SemaphoreType.DMA((2, entry_count))],
        ),
        out_shape=[
            stats_type,
            jax.ShapeDtypeStruct((block_count, width, rows), BF16),
            jax.ShapeDtypeStruct((slot_count, rows, 2 * width), BF16),
        ],
        compiler_params=params,
        cost_estimate=cost(
            2 * pair_flops * block_count * block_count * 2,
            12 * tokens * width * 2,
            HEADS * rows * rows * block_count * block_count,
        ),
        name="near_stats",
    )(
        near_ids, lengths, send_slot, token_query, cotangent, token_key, token_value, anchor_keys, anchor_values
    )
    far_rows = exchange(send_rows)

    far_stats = pl.pallas_call(
        functools.partial(far_stats_kernel, fanout=fanout),
        grid_spec=pltpu.PrefetchScalarGridSpec(
            num_scalar_prefetch=1,
            grid=(block_count,),
            in_specs=[*slot_specs((1, rows, 2 * width)), per_block, per_block],
            out_specs=whole(*slot_stats_type.shape),
        ),
        out_shape=slot_stats_type,
        compiler_params=params,
        cost_estimate=cost(
            4 * pair_flops * entry_count, 4 * entry_count * rows * width * 2, HEADS * rows * rows * entry_count
        ),
        name="far_stats",
    )(recv_slot, *([far_rows] * fanout), token_key, token_value)
    got_stats = exchange(far_stats)

    totals, total_send = pl.pallas_call(
        totals_kernel,
        grid_spec=pltpu.PrefetchScalarGridSpec(
            num_scalar_prefetch=1,
            grid=(block_count,),
            in_specs=[
                whole(*stats_type.shape),
                whole(*slot_stats_type.shape),
                per_block,
                per_block,
                whole(anchors, width),
                whole(anchors, width),
            ],
            out_specs=[block_stats, whole(*send_type.shape)],
            scratch_shapes=[pltpu.VMEM((anchors, width), F32), pltpu.VMEM((anchors, width), F32)],
        ),
        out_shape=[stats_type, send_type],
        compiler_params=params,
        cost_estimate=cost(4 * pair_flops * block_count, 2 * tokens * width * 2, HEADS * anchors * tokens),
        name="totals",
    )(send_slot, near_stats, got_stats, token_query, cotangent, anchor_keys, anchor_values)
    far_totals = exchange(total_send)
    anchor_grads = gather_anchors(far_totals[:, 2 * HEADS :, :], anchors, width)

    far_query = pl.pallas_call(
        functools.partial(far_query_kernel, fanout=fanout),
        grid_spec=pltpu.PrefetchScalarGridSpec(
            num_scalar_prefetch=1,
            grid=(block_count,),
            in_specs=[
                *slot_specs((1, rows, 2 * width)),
                *slot_specs((1, 2 * HEADS, rows)),
                per_block,
                per_block,
                turned_block,
            ],
            out_specs=whole(slot_count, rows, width),
        ),
        out_shape=jax.ShapeDtypeStruct((slot_count, rows, width), BF16),
        compiler_params=params,
        cost_estimate=cost(
            6 * pair_flops * entry_count, 5 * entry_count * rows * width * 2, HEADS * rows * rows * entry_count
        ),
        name="far_query",
    )(recv_slot, *([far_rows] * fanout), *([far_totals] * fanout), token_key, token_value, turned_keys)
    back_rows = exchange(far_query)

    dquery, key_grad, value_grad = pl.pallas_call(
        functools.partial(grads_kernel, fanout=fanout),
        grid_spec=pltpu.PrefetchScalarGridSpec(
            num_scalar_prefetch=3,
            grid=(block_count,),
            in_specs=[
                per_block,
                per_block,
                whole(tokens, width),
                whole(tokens, width),
                whole(block_count, width, rows),
                whole(anchors, width),
                whole(anchors, width),
                block_stats,
                *slot_specs((1, rows, 2 * width)),
                *slot_specs((1, 2 * HEADS, rows)),
            ],
            out_specs=[per_block, whole(tokens, width), whole(tokens, width)],
            scratch_shapes=[
                pair_scratch,
                pair_scratch,
                turned_scratch,
                turned_scratch,
                pltpu.VMEM((PAIRS, LANES, 2 * rows), F32),
                pltpu.VMEM((tokens, width), F32),
                pltpu.VMEM((tokens, width), F32),
            ],
        ),
        out_shape=[
            jax.ShapeDtypeStruct((tokens, width), F32),
            jax.ShapeDtypeStruct((tokens, width), BF16),
            jax.ShapeDtypeStruct((tokens, width), BF16),
        ],
        compiler_params=params,
        cost_estimate=cost(
            10 * pair_flops * block_count * block_count,
            8 * tokens * width * 2,
            HEADS * rows * rows * block_count * block_count,
        ),
        name="near_grads",
    )(
        near_ids, lengths, recv_slot, token_query, cotangent, token_key, token_value, turned_keys,
        anchor_keys, anchor_values, totals, *([far_rows] * fanout), *([far_totals] * fanout),
    )

    query_grad = pl.pallas_call(
        add_kernel,
        grid_spec=pltpu.PrefetchScalarGridSpec(
            num_scalar_prefetch=1,
            grid=(1,),
            in_specs=[whole(tokens, width), hbm],
            out_specs=whole(tokens, width),
            scratch_shapes=[pltpu.VMEM((entry_count, rows, width), BF16), pltpu.SemaphoreType.DMA((entry_count,))],
        ),
        out_shape=jax.ShapeDtypeStruct((tokens, width), BF16),
        compiler_params=params,
        name="add_far",
    )(send_slot, dquery, back_rows)
    return query_grad, key_grad, value_grad, anchor_grads


def gather_anchors(pieces, anchors, width):
    line_size = lax.axis_size("gx")
    own = jnp.sum(pieces.reshape(line_size, -1, *pieces.shape[1:]), axis=0)
    shares = lax.all_gather(own, ("gx", "gy"), axis=0, tiled=False)
    shares = jnp.sum(shares.reshape(line_size, -1, *own.shape), axis=1)
    piece = own.shape[1] // PAIRS
    return shares.reshape(-1, PAIRS, piece, LANES).transpose(0, 2, 1, 3).reshape(2, anchors, width)


def solution(mesh):
    split = P(("gx", "gy"), None)
    return jax.shard_map(
        shards,
        mesh=mesh,
        in_specs=(split, split, split, split, P(), P(), split, split, P(("gx", "gy"))),
        out_specs=(split, split, split, P()),
        check_vma=False,
    )
```

```python
import functools

import jax
import jax.numpy as jnp
from jax import lax
from jax.experimental import pallas as pl
from jax.experimental.pallas import tpu as pltpu
from jax.sharding import PartitionSpec as P

HEADS = 8
HEAD_DIM = 64
PAIRS = HEADS // 2
LANES = 2 * HEAD_DIM
SCALE = HEAD_DIM ** (-0.5)
LOG2E = 1.4426950408889634
EXP_SCALE = SCALE * LOG2E
CHUNKS = (4, 2, 1)
F32 = jnp.float32
BF16 = jnp.bfloat16


def pair_lanes(pair):
    return slice(pair * LANES, (pair + 1) * LANES)


def dot_nt(left, right):
    return lax.dot_general(left, right, (((1,), (1,)), ((), ())), preferred_element_type=F32)


def dot_nn(left, right):
    return jnp.dot(left, right, preferred_element_type=F32)


def dot_tn(left, right):
    return lax.dot_general(left, right, (((0,), (0,)), ((), ())), preferred_element_type=F32)


def head_masks():
    lane = lax.broadcasted_iota(jnp.int32, (1, LANES), 1)
    first = jnp.where(lane < HEAD_DIM, 1.0, 0.0)
    return first.astype(BF16), (1.0 - first).astype(BF16)


def pair_rows(rows_in, masks):
    return jnp.concatenate([rows_in * masks[0], rows_in * masks[1]], axis=0)


def stat_row(stats, pair, offset):
    at = offset + 2 * pair
    return jnp.concatenate([stats[at : at + 1], stats[at + 1 : at + 2]], axis=1)


def store_stats(stat_ref, slot, pair, log_total, delta):
    rows = log_total.shape[1] // 2
    for at, row in ((2 * pair, log_total), (HEADS + 2 * pair, delta)):
        stat_ref[slot, at : at + 1, :] = row[:, :rows]
        stat_ref[slot, at + 1 : at + 2, :] = row[:, rows:]


def first_sums(scores, dprobs):
    highest = jnp.max(scores, axis=0, keepdims=True) * EXP_SCALE
    terms = jnp.exp2(scores * EXP_SCALE - highest)
    return highest, jnp.sum(terms, axis=0, keepdims=True), jnp.sum(terms * dprobs, axis=0, keepdims=True)


def more_sums(state, scores, dprobs):
    highest, total, mass = state
    new_highest = jnp.maximum(highest, jnp.max(scores, axis=0, keepdims=True) * EXP_SCALE)
    shrink = jnp.exp2(highest - new_highest)
    terms = jnp.exp2(scores * EXP_SCALE - new_highest)
    return (
        new_highest,
        total * shrink + jnp.sum(terms, axis=0, keepdims=True),
        mass * shrink + jnp.sum(terms * dprobs, axis=0, keepdims=True),
    )


def finish_sums(state):
    highest, total, mass = state
    return highest + jnp.log(total) * LOG2E, mass / total


def weights_of(scores, dprobs, log_total, delta):
    weights = jnp.exp2(scores * EXP_SCALE - log_total)
    return weights.astype(BF16), (weights * (dprobs - delta)).astype(BF16)


def together(parts, axis):
    return parts[0] if len(parts) == 1 else jnp.concatenate(parts, axis=axis)


def staggered(items, begin, finish):
    ahead = None
    for item in items:
        begun = begin(item)
        if ahead is not None:
            finish(*ahead)
        ahead = (item, begun)
    finish(*ahead)


def block_rows_at(index, rows):
    return pl.ds(pl.multiple_of(index * rows, rows), rows)


def in_chunks(count, work, state):
    done = 0
    for size in CHUNKS:
        until = count // size
        state = lax.fori_loop(done // size, until, lambda at, held, size=size: work(at * size, size, held), state)
        done = until * size
    return state


def near_stats_kernel(
    cluster, lengths, slots, query_ref, cotan_ref, key_ref, value_ref, akey_ref, avalue_ref,
    stat_ref, keyt_ref, send_ref, qturn, oturn, sems,
):
    block = pl.program_id(0)
    block_count = pl.num_programs(0)
    rows, width = stat_ref.shape[2], query_ref.shape[1]
    fanout = slots.shape[0] // (query_ref.shape[0] // rows)

    def send_copies():
        for entry in range(slots.shape[0]):
            own = pl.ds(entry // fanout * rows, rows)
            slot = send_ref.at[slots[entry]]
            yield pltpu.make_async_copy(query_ref.at[own], slot.at[:, pl.ds(0, width)], sems.at[0, entry])
            yield pltpu.make_async_copy(cotan_ref.at[own], slot.at[:, pl.ds(width, width)], sems.at[1, entry])

    @pl.when(block == 0)
    def _():
        for copy in send_copies():
            copy.start()

    masks = head_masks()
    own = block_rows_at(block, rows)
    start = []
    for pair in range(PAIRS):
        lanes = pair_lanes(pair)
        qturn[pair] = pair_rows(query_ref[own, lanes], masks).T
        oturn[pair] = pair_rows(cotan_ref[own, lanes], masks).T
        keyt_ref[0, lanes, :] = key_ref[own, lanes].T
        start.append(
            first_sums(dot_nn(akey_ref[:, lanes], qturn[pair]), dot_nn(avalue_ref[:, lanes], oturn[pair]))
        )

    def work(first, count, states):
        spots = [
            block_rows_at(cluster[block, first + which], rows) for which in range(count)
        ]
        states = list(states)

        def begin(pair):
            lanes = pair_lanes(pair)
            return (
                dot_nn(together([key_ref[at, lanes] for at in spots], 0), qturn[pair]),
                dot_nn(together([value_ref[at, lanes] for at in spots], 0), oturn[pair]),
            )

        def finish(pair, tiles):
            states[pair] = more_sums(states[pair], *tiles)

        staggered(range(PAIRS), begin, finish)
        return tuple(states)

    states = in_chunks(lengths[block], work, tuple(start))
    for pair in range(PAIRS):
        store_stats(stat_ref, 0, pair, *finish_sums(states[pair]))

    @pl.when(block == block_count - 1)
    def _():
        for copy in send_copies():
            copy.wait()


def far_tiles(far_ref, keys, values, pair, masks):
    lanes = pair_lanes(pair)
    width = far_ref.shape[2] // 2
    queries = pair_rows(far_ref[0, :, lanes], masks)
    cotans = pair_rows(far_ref[0, :, width + lanes.start : width + lanes.stop], masks)
    return dot_nt(keys, queries), dot_nt(values, cotans), queries, cotans


def far_stats_kernel(slots, *refs, fanout):
    far_refs, (key_ref, value_ref, stat_ref) = refs[:fanout], refs[fanout:]
    masks = head_masks()
    step = pl.program_id(0)

    def begin(item):
        which, pair = item
        return far_tiles(far_refs[which], key_ref[:, pair_lanes(pair)], value_ref[:, pair_lanes(pair)], pair, masks)

    def finish(item, tiles):
        which, pair = item
        store_stats(stat_ref, slots[step * fanout + which], pair, *finish_sums(first_sums(*tiles[:2])))

    staggered([(which, pair) for which in range(fanout) for pair in range(PAIRS)], begin, finish)


def totals_kernel(
    slots, near_ref, far_ref, query_ref, cotan_ref, akey_ref, avalue_ref, total_ref, send_ref, key_acc, value_acc
):
    block = pl.program_id(0)
    block_count = pl.num_programs(0)
    fanout = slots.shape[0] // near_ref.shape[0]

    @pl.when(block == 0)
    def _():
        key_acc[...] = jnp.zeros_like(key_acc)
        value_acc[...] = jnp.zeros_like(value_acc)

    mine = [slots[block * fanout + which] for which in range(fanout)]
    parts = [near_ref[block]] + [far_ref[slot] for slot in mine]
    logs = [part[:HEADS] for part in parts]
    highest = functools.reduce(jnp.maximum, logs)
    shares = [jnp.exp2(log - highest) for log in logs]
    total = sum(shares)
    mass = sum(share * part[HEADS:] for share, part in zip(shares, parts))
    stats = jnp.concatenate([highest + jnp.log(total) * LOG2E, mass / total], axis=0)
    total_ref[0] = stats
    for slot in mine:
        send_ref[slot, : 2 * HEADS, :] = stats

    masks = head_masks()

    def begin(pair):
        lanes = pair_lanes(pair)
        qpair = pair_rows(query_ref[:, lanes], masks)
        opair = pair_rows(cotan_ref[:, lanes], masks)
        return dot_nt(akey_ref[:, lanes], qpair), dot_nt(avalue_ref[:, lanes], opair), qpair, opair

    def finish(pair, tiles):
        scores, dprobs, qpair, opair = tiles
        weights, dscore = weights_of(scores, dprobs, stat_row(stats, pair, 0), stat_row(stats, pair, HEADS))
        key_acc[:, pair_lanes(pair)] += dot_nn(dscore, qpair)
        value_acc[:, pair_lanes(pair)] += dot_nn(weights, opair)

    staggered(range(PAIRS), begin, finish)

    @pl.when(block == block_count - 1)
    def _():
        slot_count = send_ref.shape[0]
        piece = 2 * key_acc.shape[0] // slot_count
        for slot in range(slot_count):
            acc, factor = (key_acc, SCALE) if slot < slot_count // 2 else (value_acc, 1.0)
            first = slot % (slot_count // 2) * piece
            for pair in range(PAIRS):
                at = 2 * HEADS + pair * piece
                send_ref[slot, at : at + piece, :] = acc[first : first + piece, pair_lanes(pair)] * factor


def unpair_turned(both):
    rows = both.shape[1] // 2
    feature = lax.broadcasted_iota(jnp.int32, (LANES, rows), 0)
    return jnp.where(feature < HEAD_DIM, both[:, :rows], both[:, rows:]).T


def far_query_kernel(slots, *refs, fanout):
    far_refs, stat_refs, refs = refs[:fanout], refs[fanout : 2 * fanout], refs[2 * fanout :]
    key_ref, value_ref, keyt_ref, out_ref = refs
    masks = head_masks()
    step = pl.program_id(0)
    stats = [stat_ref[0] for stat_ref in stat_refs]

    def begin(item):
        which, pair = item
        return far_tiles(far_refs[which], key_ref[:, pair_lanes(pair)], value_ref[:, pair_lanes(pair)], pair, masks)

    def finish(item, tiles):
        which, pair = item
        logs, deltas = stat_row(stats[which], pair, 0), stat_row(stats[which], pair, HEADS)
        _, dscore = weights_of(*tiles[:2], logs, deltas)
        far_grad = unpair_turned(dot_nn(keyt_ref[0, pair_lanes(pair), :], dscore)) * SCALE
        out_ref[slots[step * fanout + which], :, pair_lanes(pair)] = far_grad.astype(BF16)

    staggered([(which, pair) for which in range(fanout) for pair in range(PAIRS)], begin, finish)


def grads_kernel(
    cluster, lengths, slots, query_ref, cotan_ref, key_ref, value_ref, keyt_ref, akey_ref, avalue_ref, total_ref,
    *refs, fanout,
):
    far_refs, stat_refs, refs = refs[:fanout], refs[fanout : 2 * fanout], refs[2 * fanout :]
    dquery_ref, dkey_ref, dvalue_ref, qpair, opair, qturn, oturn, dq_acc, dk_acc, dv_acc = refs
    block = pl.program_id(0)
    block_count = pl.num_programs(0)
    rows, width = query_ref.shape

    @pl.when(block == 0)
    def _():
        dk_acc[...] = jnp.zeros_like(dk_acc)
        dv_acc[...] = jnp.zeros_like(dv_acc)

    masks = head_masks()
    stats = total_ref[0]
    logs = [stat_row(stats, pair, 0) for pair in range(PAIRS)]
    deltas = [stat_row(stats, pair, HEADS) for pair in range(PAIRS)]
    for pair in range(PAIRS):
        lanes = pair_lanes(pair)
        qpair[pair] = pair_rows(query_ref[:, lanes], masks)
        opair[pair] = pair_rows(cotan_ref[:, lanes], masks)
        qturn[pair] = qpair[pair].T
        oturn[pair] = opair[pair].T
        akeys = akey_ref[:, lanes]
        scores = dot_nn(akeys, qturn[pair])
        dprobs = dot_nn(avalue_ref[:, lanes], oturn[pair])
        _, dscore = weights_of(scores, dprobs, logs[pair], deltas[pair])
        dq_acc[pair] = dot_tn(akeys, dscore)

    def work(first, count, carry):
        ids = [cluster[block, first + which] for which in range(count)]
        spots = [block_rows_at(index, rows) for index in ids]

        def begin(pair):
            lanes = pair_lanes(pair)
            return (
                dot_nn(together([key_ref[at, lanes] for at in spots], 0), qturn[pair]),
                dot_nn(together([value_ref[at, lanes] for at in spots], 0), oturn[pair]),
            )

        def finish(pair, tiles):
            lanes = pair_lanes(pair)
            weights, dscore = weights_of(*tiles, logs[pair], deltas[pair])
            key_part = dot_nn(dscore, qpair[pair])
            value_part = dot_nn(weights, opair[pair])
            for which, at in enumerate(spots):
                part = slice(which * rows, (which + 1) * rows)
                dk_acc[at, lanes] += key_part[part]
                dv_acc[at, lanes] += value_part[part]
            dq_acc[pair] += dot_nn(together([keyt_ref[index, lanes, :] for index in ids], 1), dscore)

        staggered(range(PAIRS), begin, finish)
        return carry

    in_chunks(lengths[block], work, 0)
    for pair in range(PAIRS):
        dquery_ref[:, pair_lanes(pair)] = unpair_turned(dq_acc[pair]) * SCALE

    own = block_rows_at(block, rows)
    far_stats = [stat_ref[0] for stat_ref in stat_refs]

    def begin_far(pair):
        keys, values = key_ref[own, pair_lanes(pair)], value_ref[own, pair_lanes(pair)]
        return [far_tiles(far_ref, keys, values, pair, masks) for far_ref in far_refs]

    def finish_far(pair, tiles):
        lanes = pair_lanes(pair)
        both = [
            weights_of(*tile[:2], stat_row(far_stat, pair, 0), stat_row(far_stat, pair, HEADS))
            for tile, far_stat in zip(tiles, far_stats)
        ]
        dscores, weights = [dscore for _, dscore in both], [weights for weights, _ in both]
        dk_acc[own, lanes] += dot_nn(together(dscores, 1), together([tile[2] for tile in tiles], 0))
        dv_acc[own, lanes] += dot_nn(together(weights, 1), together([tile[3] for tile in tiles], 0))

    staggered(range(PAIRS), begin_far, finish_far)

    @pl.when(block == block_count - 1)
    def _():
        dkey_ref[...] = (dk_acc[...] * SCALE).astype(BF16)
        dvalue_ref[...] = dv_acc[...].astype(BF16)


def add_kernel(slots, near_ref, back_ref, out_ref, landed, sems):
    entry_count = slots.shape[0]
    rows = landed.shape[1]
    fanout = entry_count // (near_ref.shape[0] // rows)
    copies = [
        pltpu.make_async_copy(back_ref.at[slots[entry]], landed.at[entry], sems.at[entry])
        for entry in range(entry_count)
    ]
    for copy in copies:
        copy.start()
    for block in range(entry_count // fanout):
        own = pl.ds(block * rows, rows)
        total = near_ref[own, :]
        for entry in range(block * fanout, (block + 1) * fanout):
            copies[entry].wait()
            total = total + landed[entry].astype(F32)
        out_ref[own, :] = total.astype(BF16)


def cost(flops, bytes_accessed, exps):
    return pl.CostEstimate(flops=int(flops), bytes_accessed=int(bytes_accessed), transcendentals=int(exps))


def shards(token_query, token_key, token_value, cotangent, anchor_keys, anchor_values, partner, cluster, lengths):
    block_count, fanout = partner.shape
    tokens, width = token_query.shape
    rows = tokens // block_count
    anchors = anchor_keys.shape[0]
    line_size = lax.axis_size("gx")
    row_size = lax.axis_size("gy")
    entry_count = block_count * fanout
    capacity = 2 * ((entry_count // 2 + line_size - 2) // (line_size - 1))
    slot_count = line_size * capacity
    params = pltpu.CompilerParams(vmem_limit_bytes=40 * 1024 * 1024)
    large_params = pltpu.CompilerParams(vmem_limit_bytes=60 * 1024 * 1024)

    entries = jnp.arange(entry_count, dtype=jnp.int32)
    targets = partner.reshape(-1)
    peer_index = targets // block_count // row_size
    ordering = targets * fanout + entries % fanout
    same_peer = peer_index[:, None] == peer_index[None, :]
    recv_slot = peer_index * capacity + jnp.sum(same_peer & (entries[None, :] < entries[:, None]), axis=1)
    send_slot = peer_index * capacity + jnp.sum(same_peer & (ordering[None, :] < ordering[:, None]), axis=1)
    recv_slot = recv_slot.astype(jnp.int32)
    send_slot = send_slot.astype(jnp.int32)

    def exchange(rows_out):
        return lax.all_to_all(rows_out, "gx", split_axis=0, concat_axis=0, tiled=True)

    pair_flops = 2 * rows * rows * width
    whole = lambda *shape: pl.BlockSpec(shape, lambda step, *_: (0,) * len(shape))
    per_block = pl.BlockSpec((rows, width), lambda step, *_: (step, 0))
    block_stats = pl.BlockSpec((1, 2 * HEADS, rows), lambda step, *_: (step, 0, 0))
    turned_block = pl.BlockSpec((1, width, rows), lambda step, *_: (step, 0, 0))
    hbm = pl.BlockSpec(memory_space=pl.ANY)
    stats_type = jax.ShapeDtypeStruct((block_count, 2 * HEADS, rows), F32)
    slot_stats_type = jax.ShapeDtypeStruct((slot_count, 2 * HEADS, rows), F32)
    send_type = jax.ShapeDtypeStruct((slot_count, 4 * HEADS, rows), F32)
    pair_scratch = pltpu.VMEM((PAIRS, 2 * rows, LANES), BF16)
    turned_scratch = pltpu.VMEM((PAIRS, LANES, 2 * rows), BF16)

    def slot_specs(shape):
        def spec(which):
            return pl.BlockSpec(shape, lambda step, *scalars: (scalars[-1][step * fanout + which], 0, 0))

        return [spec(which) for which in range(fanout)]

    near_stats, turned_keys, send_rows = pl.pallas_call(
        near_stats_kernel,
        grid_spec=pltpu.PrefetchScalarGridSpec(
            num_scalar_prefetch=3,
            grid=(block_count,),
            in_specs=[
                whole(tokens, width),
                whole(tokens, width),
                whole(tokens, width),
                whole(tokens, width),
                whole(anchors, width),
                whole(anchors, width),
            ],
            out_specs=[block_stats, turned_block, hbm],
            scratch_shapes=[turned_scratch, turned_scratch, pltpu.SemaphoreType.DMA((2, entry_count))],
        ),
        out_shape=[
            stats_type,
            jax.ShapeDtypeStruct((block_count, width, rows), BF16),
            jax.ShapeDtypeStruct((slot_count, rows, 2 * width), BF16),
        ],
        compiler_params=large_params,
        cost_estimate=cost(
            2 * pair_flops * block_count * block_count * 2,
            12 * tokens * width * 2,
            HEADS * rows * rows * block_count * block_count,
        ),
        name="near_stats",
    )(
        cluster, lengths, send_slot, token_query, cotangent, token_key, token_value, anchor_keys, anchor_values
    )
    far_rows = exchange(send_rows)

    far_stats = pl.pallas_call(
        functools.partial(far_stats_kernel, fanout=fanout),
        grid_spec=pltpu.PrefetchScalarGridSpec(
            num_scalar_prefetch=1,
            grid=(block_count,),
            in_specs=[*slot_specs((1, rows, 2 * width)), per_block, per_block],
            out_specs=whole(*slot_stats_type.shape),
        ),
        out_shape=slot_stats_type,
        compiler_params=params,
        cost_estimate=cost(
            4 * pair_flops * entry_count, 4 * entry_count * rows * width * 2, HEADS * rows * rows * entry_count
        ),
        name="far_stats",
    )(recv_slot, *([far_rows] * fanout), token_key, token_value)
    got_stats = exchange(far_stats)

    totals, total_send = pl.pallas_call(
        totals_kernel,
        grid_spec=pltpu.PrefetchScalarGridSpec(
            num_scalar_prefetch=1,
            grid=(block_count,),
            in_specs=[
                whole(*stats_type.shape),
                whole(*slot_stats_type.shape),
                per_block,
                per_block,
                whole(anchors, width),
                whole(anchors, width),
            ],
            out_specs=[block_stats, whole(*send_type.shape)],
            scratch_shapes=[pltpu.VMEM((anchors, width), F32), pltpu.VMEM((anchors, width), F32)],
        ),
        out_shape=[stats_type, send_type],
        compiler_params=params,
        cost_estimate=cost(4 * pair_flops * block_count, 2 * tokens * width * 2, HEADS * anchors * tokens),
        name="totals",
    )(send_slot, near_stats, got_stats, token_query, cotangent, anchor_keys, anchor_values)
    far_totals = exchange(total_send)
    far_query = pl.pallas_call(
        functools.partial(far_query_kernel, fanout=fanout),
        grid_spec=pltpu.PrefetchScalarGridSpec(
            num_scalar_prefetch=1,
            grid=(block_count,),
            in_specs=[
                *slot_specs((1, rows, 2 * width)),
                *slot_specs((1, 2 * HEADS, rows)),
                per_block,
                per_block,
                turned_block,
            ],
            out_specs=whole(slot_count, rows, width),
        ),
        out_shape=jax.ShapeDtypeStruct((slot_count, rows, width), BF16),
        compiler_params=params,
        cost_estimate=cost(
            6 * pair_flops * entry_count, 5 * entry_count * rows * width * 2, HEADS * rows * rows * entry_count
        ),
        name="far_query",
    )(recv_slot, *([far_rows] * fanout), *([far_totals] * fanout), token_key, token_value, turned_keys)
    far_query, anchor_pieces = lax.optimization_barrier((far_query, far_totals))
    back_rows = exchange(far_query)
    anchor_share = sum_share(anchor_pieces[:, 2 * HEADS :, :])

    dquery, key_grad, value_grad = pl.pallas_call(
        functools.partial(grads_kernel, fanout=fanout),
        grid_spec=pltpu.PrefetchScalarGridSpec(
            num_scalar_prefetch=3,
            grid=(block_count,),
            in_specs=[
                per_block,
                per_block,
                whole(tokens, width),
                whole(tokens, width),
                whole(block_count, width, rows),
                whole(anchors, width),
                whole(anchors, width),
                block_stats,
                *slot_specs((1, rows, 2 * width)),
                *slot_specs((1, 2 * HEADS, rows)),
            ],
            out_specs=[per_block, whole(tokens, width), whole(tokens, width)],
            scratch_shapes=[
                pair_scratch,
                pair_scratch,
                turned_scratch,
                turned_scratch,
                pltpu.VMEM((PAIRS, LANES, 2 * rows), F32),
                pltpu.VMEM((tokens, width), F32),
                pltpu.VMEM((tokens, width), F32),
            ],
        ),
        out_shape=[
            jax.ShapeDtypeStruct((tokens, width), F32),
            jax.ShapeDtypeStruct((tokens, width), BF16),
            jax.ShapeDtypeStruct((tokens, width), BF16),
        ],
        compiler_params=large_params,
        cost_estimate=cost(
            10 * pair_flops * block_count * block_count,
            8 * tokens * width * 2,
            HEADS * rows * rows * block_count * block_count,
        ),
        name="near_grads",
    )(
        cluster, lengths, recv_slot, token_query, cotangent, token_key, token_value, turned_keys,
        anchor_keys, anchor_values, totals, *([far_rows] * fanout), *([far_totals] * fanout),
    )

    back_rows, anchor_share, dquery = lax.optimization_barrier((back_rows, anchor_share, dquery))
    anchor_grads = gather_anchors(anchor_share, anchors, width)
    query_grad = pl.pallas_call(
        add_kernel,
        grid_spec=pltpu.PrefetchScalarGridSpec(
            num_scalar_prefetch=1,
            grid=(1,),
            in_specs=[whole(tokens, width), hbm],
            out_specs=whole(tokens, width),
            scratch_shapes=[pltpu.VMEM((entry_count, rows, width), BF16), pltpu.SemaphoreType.DMA((entry_count,))],
        ),
        out_shape=jax.ShapeDtypeStruct((tokens, width), BF16),
        compiler_params=params,
        name="add_far",
    )(send_slot, dquery, back_rows)
    return query_grad, key_grad, value_grad, anchor_grads


def sum_share(pieces):
    line_size, row_size = lax.axis_size("gx"), lax.axis_size("gy")
    share = jnp.sum(pieces.reshape(line_size, -1, *pieces.shape[1:]), axis=0)
    for step in range(row_size.bit_length() - 1):
        share = share + lax.ppermute(share, "gy", [(at, at ^ (1 << step)) for at in range(row_size)])
    return share


def gather_anchors(share, anchors, width):
    line_size = lax.axis_size("gx")
    copies = jnp.broadcast_to(share[None], (line_size, *share.shape))
    shares = lax.all_to_all(copies, "gx", split_axis=0, concat_axis=0, tiled=True)
    piece = share.shape[1] // PAIRS
    return shares.reshape(-1, PAIRS, piece, LANES).transpose(0, 2, 1, 3).reshape(2, anchors, width)


def solution(mesh):
    split = P(("gx", "gy"), None)
    return jax.shard_map(
        shards,
        mesh=mesh,
        in_specs=(split, split, split, split, P(), P(), split, split, P(("gx", "gy"))),
        out_specs=(split, split, split, P()),
        check_vma=False,
    )
```

```python
import functools

import jax
import jax.numpy as jnp
from jax import lax
from jax.experimental import pallas as pl
from jax.experimental.pallas import tpu as pltpu
from jax.sharding import PartitionSpec as P

HEADS = 8
HEAD_DIM = 64
PAIRS = HEADS // 2
LANES = 2 * HEAD_DIM
SCALE = HEAD_DIM ** (-0.5)
LOG2E = 1.4426950408889634
EXP_SCALE = SCALE * LOG2E
CHUNKS = (4, 2, 1)
F32 = jnp.float32
BF16 = jnp.bfloat16


def pair_lanes(pair):
    return slice(pair * LANES, (pair + 1) * LANES)


def dot_nt(left, right):
    return lax.dot_general(left, right, (((1,), (1,)), ((), ())), preferred_element_type=F32)


def dot_nn(left, right):
    return jnp.dot(left, right, preferred_element_type=F32)


def dot_tn(left, right):
    return lax.dot_general(left, right, (((0,), (0,)), ((), ())), preferred_element_type=F32)


def head_masks():
    lane = lax.broadcasted_iota(jnp.int32, (1, LANES), 1)
    first = jnp.where(lane < HEAD_DIM, 1.0, 0.0)
    return first.astype(BF16), (1.0 - first).astype(BF16)


def pair_rows(rows_in, masks):
    return jnp.concatenate([rows_in * masks[0], rows_in * masks[1]], axis=0)


def turned_masks(rows):
    feature = lax.broadcasted_iota(jnp.int32, (LANES, rows), 0)
    first = jnp.where(feature < HEAD_DIM, 1.0, 0.0)
    return first.astype(BF16), (1.0 - first).astype(BF16)


def turned_pair(rows_in, masks):
    turned = rows_in.T
    return jnp.concatenate([turned * masks[0], turned * masks[1]], axis=1)


def stat_row(stats, pair, offset):
    at = offset + 2 * pair
    return jnp.concatenate([stats[at : at + 1], stats[at + 1 : at + 2]], axis=1)


def store_stats(stat_ref, slot, pair, log_total, delta):
    rows = log_total.shape[1] // 2
    for at, row in ((2 * pair, log_total), (HEADS + 2 * pair, delta)):
        stat_ref[slot, at : at + 1, :] = row[:, :rows]
        stat_ref[slot, at + 1 : at + 2, :] = row[:, rows:]


def first_sums(scores, dprobs):
    highest = jnp.max(scores, axis=0, keepdims=True) * EXP_SCALE
    terms = jnp.exp2(scores * EXP_SCALE - highest)
    return highest, jnp.sum(terms, axis=0, keepdims=True), jnp.sum(terms * dprobs, axis=0, keepdims=True)


def more_sums(state, scores, dprobs):
    highest, total, mass = state
    new_highest = jnp.maximum(highest, jnp.max(scores, axis=0, keepdims=True) * EXP_SCALE)
    shrink = jnp.exp2(highest - new_highest)
    terms = jnp.exp2(scores * EXP_SCALE - new_highest)
    return (
        new_highest,
        total * shrink + jnp.sum(terms, axis=0, keepdims=True),
        mass * shrink + jnp.sum(terms * dprobs, axis=0, keepdims=True),
    )


def finish_sums(state):
    highest, total, mass = state
    return highest + jnp.log(total) * LOG2E, mass / total


def weights_of(scores, dprobs, log_total, delta):
    weights = jnp.exp2(scores * EXP_SCALE - log_total)
    return weights.astype(BF16), (weights * (dprobs - delta)).astype(BF16)


def together(parts, axis):
    return parts[0] if len(parts) == 1 else jnp.concatenate(parts, axis=axis)


def staggered(items, begin, finish):
    ahead = None
    for item in items:
        begun = begin(item)
        if ahead is not None:
            finish(*ahead)
        ahead = (item, begun)
    finish(*ahead)


def block_rows_at(index, rows):
    return pl.ds(pl.multiple_of(index * rows, rows), rows)


def in_chunks(count, work, state):
    done = 0
    for size in CHUNKS:
        until = count // size
        state = lax.fori_loop(done // size, until, lambda at, held, size=size: work(at * size, size, held), state)
        done = until * size
    return state


def entry_slots(partner, block_count, row_size, capacity):
    fanout = partner.shape[0]
    entry_count = block_count * fanout
    targets = [partner[entry % fanout, entry // fanout] for entry in range(entry_count)]
    peers = [target // (block_count * row_size) for target in targets]
    order = [target * fanout + entry % fanout for entry, target in enumerate(targets)]
    sent_before, got_before = [0] * entry_count, [0] * entry_count
    for left in range(entry_count):
        for right in range(left + 1, entry_count):
            same = (peers[left] == peers[right]).astype(jnp.int32)
            swapped = jnp.where(order[right] < order[left], same, 0)
            sent_before[left] = sent_before[left] + swapped
            sent_before[right] = sent_before[right] + (same - swapped)
            got_before[right] = got_before[right] + same
    firsts = [peer * capacity for peer in peers]
    sent = [first + count for first, count in zip(firsts, sent_before)]
    return sent, [first + count for first, count in zip(firsts, got_before)]


def near_stats_kernel(
    cluster, lengths, partner, query_ref, cotan_ref, key_ref, value_ref, akey_ref, avalue_ref,
    stat_ref, keyt_ref, send_ref, send_slot, recv_slot, qturn, oturn, sems, *, row_size, capacity,
):
    block = pl.program_id(0)
    block_count = pl.num_programs(0)
    rows, width = stat_ref.shape[2], query_ref.shape[1]
    fanout = partner.shape[0]

    def send_copies(slots):
        for entry, slot in enumerate(slots):
            own = pl.ds(entry // fanout * rows, rows)
            into = send_ref.at[slot]
            yield pltpu.make_async_copy(query_ref.at[own], into.at[:, pl.ds(0, width)], sems.at[0, entry])
            yield pltpu.make_async_copy(cotan_ref.at[own], into.at[:, pl.ds(width, width)], sems.at[1, entry])

    @pl.when(block == 0)
    def _():
        sent, received = entry_slots(partner, block_count_of(query_ref, rows), row_size, capacity)
        for copy in send_copies(sent):
            copy.start()
        for entry in range(len(sent)):
            send_slot[entry] = sent[entry]
            recv_slot[entry] = received[entry]

    masks = turned_masks(rows)
    own = block_rows_at(block, rows)
    start = [None] * PAIRS

    def begin_anchors(pair):
        lanes = pair_lanes(pair)
        queries = turned_pair(query_ref[own, lanes], masks)
        cotans = turned_pair(cotan_ref[own, lanes], masks)
        qturn[pair] = queries
        oturn[pair] = cotans
        keyt_ref[0, lanes, :] = key_ref[own, lanes].T
        return dot_nn(akey_ref[:, lanes], queries), dot_nn(avalue_ref[:, lanes], cotans)

    def finish_anchors(pair, tiles):
        start[pair] = first_sums(*tiles)

    staggered(range(PAIRS), begin_anchors, finish_anchors)

    def work(first, count, states):
        spots = [
            block_rows_at(cluster[block, first + which], rows) for which in range(count)
        ]
        states = list(states)

        def begin(pair):
            lanes = pair_lanes(pair)
            return (
                dot_nn(together([key_ref[at, lanes] for at in spots], 0), qturn[pair]),
                dot_nn(together([value_ref[at, lanes] for at in spots], 0), oturn[pair]),
            )

        def finish(pair, tiles):
            states[pair] = more_sums(states[pair], *tiles)

        staggered(range(PAIRS), begin, finish)
        return tuple(states)

    states = in_chunks(lengths[block], work, tuple(start))
    for pair in range(PAIRS):
        store_stats(stat_ref, 0, pair, *finish_sums(states[pair]))

    @pl.when(block == block_count - 1)
    def _():
        for copy in send_copies([0] * (block_count_of(query_ref, rows) * fanout)):
            copy.wait()


def block_count_of(rows_ref, rows):
    return rows_ref.shape[0] // rows


def far_tiles(far_ref, keys, values, pair, masks):
    lanes = pair_lanes(pair)
    width = far_ref.shape[2] // 2
    queries = pair_rows(far_ref[0, :, lanes], masks)
    cotans = pair_rows(far_ref[0, :, width + lanes.start : width + lanes.stop], masks)
    return dot_nt(keys, queries), dot_nt(values, cotans), queries, cotans


def far_stats_kernel(slots, *refs, fanout):
    far_refs, (key_ref, value_ref, stat_ref) = refs[:fanout], refs[fanout:]
    masks = head_masks()
    step = pl.program_id(0)

    def begin(item):
        which, pair = item
        return far_tiles(far_refs[which], key_ref[:, pair_lanes(pair)], value_ref[:, pair_lanes(pair)], pair, masks)

    def finish(item, tiles):
        which, pair = item
        store_stats(stat_ref, slots[step * fanout + which], pair, *finish_sums(first_sums(*tiles[:2])))

    staggered([(which, pair) for which in range(fanout) for pair in range(PAIRS)], begin, finish)


def totals_kernel(
    slots, near_ref, far_ref, query_ref, cotan_ref, akey_ref, avalue_ref, total_ref, send_ref, key_acc, value_acc
):
    block = pl.program_id(0)
    block_count = pl.num_programs(0)
    fanout = slots.shape[0] // near_ref.shape[0]

    @pl.when(block == 0)
    def _():
        key_acc[...] = jnp.zeros_like(key_acc)
        value_acc[...] = jnp.zeros_like(value_acc)

    mine = [slots[block * fanout + which] for which in range(fanout)]
    parts = [near_ref[block]] + [far_ref[slot] for slot in mine]
    logs = [part[:HEADS] for part in parts]
    highest = functools.reduce(jnp.maximum, logs)
    shares = [jnp.exp2(log - highest) for log in logs]
    total = sum(shares)
    mass = sum(share * part[HEADS:] for share, part in zip(shares, parts))
    stats = jnp.concatenate([highest + jnp.log(total) * LOG2E, mass / total], axis=0)
    total_ref[0] = stats
    for slot in mine:
        send_ref[slot, : 2 * HEADS, :] = stats

    masks = head_masks()

    def begin(pair):
        lanes = pair_lanes(pair)
        qpair = pair_rows(query_ref[:, lanes], masks)
        opair = pair_rows(cotan_ref[:, lanes], masks)
        return dot_nt(akey_ref[:, lanes], qpair), dot_nt(avalue_ref[:, lanes], opair), qpair, opair

    def finish(pair, tiles):
        scores, dprobs, qpair, opair = tiles
        weights, dscore = weights_of(scores, dprobs, stat_row(stats, pair, 0), stat_row(stats, pair, HEADS))
        key_acc[:, pair_lanes(pair)] += dot_nn(dscore, qpair)
        value_acc[:, pair_lanes(pair)] += dot_nn(weights, opair)

    staggered(range(PAIRS), begin, finish)

    @pl.when(block == block_count - 1)
    def _():
        slot_count = send_ref.shape[0]
        piece = 2 * key_acc.shape[0] // slot_count
        for slot in range(slot_count):
            acc, factor = (key_acc, SCALE) if slot < slot_count // 2 else (value_acc, 1.0)
            first = slot % (slot_count // 2) * piece
            for pair in range(PAIRS):
                at = 2 * HEADS + pair * piece
                send_ref[slot, at : at + piece, :] = acc[first : first + piece, pair_lanes(pair)] * factor


def unpair_turned(both):
    rows = both.shape[1] // 2
    feature = lax.broadcasted_iota(jnp.int32, (LANES, rows), 0)
    return jnp.where(feature < HEAD_DIM, both[:, :rows], both[:, rows:]).T


def far_query_kernel(slots, *refs, fanout):
    far_refs, stat_refs, refs = refs[:fanout], refs[fanout : 2 * fanout], refs[2 * fanout :]
    key_ref, value_ref, keyt_ref, out_ref = refs
    masks = head_masks()
    step = pl.program_id(0)
    stats = [stat_ref[0] for stat_ref in stat_refs]

    def begin(item):
        which, pair = item
        return far_tiles(far_refs[which], key_ref[:, pair_lanes(pair)], value_ref[:, pair_lanes(pair)], pair, masks)

    def finish(item, tiles):
        which, pair = item
        logs, deltas = stat_row(stats[which], pair, 0), stat_row(stats[which], pair, HEADS)
        _, dscore = weights_of(*tiles[:2], logs, deltas)
        far_grad = unpair_turned(dot_nn(keyt_ref[0, pair_lanes(pair), :], dscore)) * SCALE
        out_ref[slots[step * fanout + which], :, pair_lanes(pair)] = far_grad.astype(BF16)

    staggered([(which, pair) for which in range(fanout) for pair in range(PAIRS)], begin, finish)


def grads_kernel(
    cluster, lengths, slots, query_ref, cotan_ref, key_ref, value_ref, keyt_ref, akey_ref, avalue_ref, total_ref,
    *refs, fanout,
):
    far_refs, stat_refs, refs = refs[:fanout], refs[fanout : 2 * fanout], refs[2 * fanout :]
    dquery_ref, dkey_ref, dvalue_ref, qpair, opair, qturn, oturn, aturn, dq_acc, dk_acc, dv_acc = refs
    block = pl.program_id(0)
    block_count = pl.num_programs(0)
    rows, width = query_ref.shape

    @pl.when(block == 0)
    def _():
        dk_acc[...] = jnp.zeros_like(dk_acc)
        dv_acc[...] = jnp.zeros_like(dv_acc)
        for pair in range(PAIRS):
            aturn[pair_lanes(pair), :] = akey_ref[:, pair_lanes(pair)].T

    masks = head_masks()
    lane_masks = turned_masks(rows)
    stats = total_ref[0]
    logs = [stat_row(stats, pair, 0) for pair in range(PAIRS)]
    deltas = [stat_row(stats, pair, HEADS) for pair in range(PAIRS)]

    def begin_anchors(pair):
        lanes = pair_lanes(pair)
        queries = turned_pair(query_ref[:, lanes], lane_masks)
        cotans = turned_pair(cotan_ref[:, lanes], lane_masks)
        qturn[pair] = queries
        oturn[pair] = cotans
        qpair[pair] = pair_rows(query_ref[:, lanes], masks)
        opair[pair] = pair_rows(cotan_ref[:, lanes], masks)
        return dot_nn(akey_ref[:, lanes], queries), dot_nn(avalue_ref[:, lanes], cotans)

    def finish_anchors(pair, tiles):
        _, dscore = weights_of(*tiles, logs[pair], deltas[pair])
        dq_acc[pair] = dot_nn(aturn[pair_lanes(pair), :], dscore)

    staggered(range(PAIRS), begin_anchors, finish_anchors)

    def work(first, count, carry):
        ids = [cluster[block, first + which] for which in range(count)]
        spots = [block_rows_at(index, rows) for index in ids]

        def begin(pair):
            lanes = pair_lanes(pair)
            return (
                dot_nn(together([key_ref[at, lanes] for at in spots], 0), qturn[pair]),
                dot_nn(together([value_ref[at, lanes] for at in spots], 0), oturn[pair]),
            )

        def finish(pair, tiles):
            lanes = pair_lanes(pair)
            weights, dscore = weights_of(*tiles, logs[pair], deltas[pair])
            key_part = dot_nn(dscore, qpair[pair])
            value_part = dot_nn(weights, opair[pair])
            for which, at in enumerate(spots):
                part = slice(which * rows, (which + 1) * rows)
                dk_acc[at, lanes] += key_part[part]
                dv_acc[at, lanes] += value_part[part]
            dq_acc[pair] += dot_nn(together([keyt_ref[index, lanes, :] for index in ids], 1), dscore)

        staggered(range(PAIRS), begin, finish)
        return carry

    in_chunks(lengths[block], work, 0)
    for pair in range(PAIRS):
        dquery_ref[:, pair_lanes(pair)] = unpair_turned(dq_acc[pair]) * SCALE

    own = block_rows_at(block, rows)
    far_stats = [stat_ref[0] for stat_ref in stat_refs]

    def begin_far(pair):
        keys, values = key_ref[own, pair_lanes(pair)], value_ref[own, pair_lanes(pair)]
        return [far_tiles(far_ref, keys, values, pair, masks) for far_ref in far_refs]

    def finish_far(pair, tiles):
        lanes = pair_lanes(pair)
        both = [
            weights_of(*tile[:2], stat_row(far_stat, pair, 0), stat_row(far_stat, pair, HEADS))
            for tile, far_stat in zip(tiles, far_stats)
        ]
        dscores, weights = [dscore for _, dscore in both], [weights for weights, _ in both]
        dk_acc[own, lanes] += dot_nn(together(dscores, 1), together([tile[2] for tile in tiles], 0))
        dv_acc[own, lanes] += dot_nn(together(weights, 1), together([tile[3] for tile in tiles], 0))

    staggered(range(PAIRS), begin_far, finish_far)

    @pl.when(block == block_count - 1)
    def _():
        dkey_ref[...] = (dk_acc[...] * SCALE).astype(BF16)
        dvalue_ref[...] = dv_acc[...].astype(BF16)


def add_kernel(slots, near_ref, back_ref, out_ref, near, landed, ready, near_sems, back_sems, out_sems):
    entry_count, rows = landed.shape[:2]
    block_count = near.shape[0]
    fanout = entry_count // block_count
    nears = [
        pltpu.make_async_copy(near_ref.at[pl.ds(block * rows, rows)], near.at[block], near_sems.at[block])
        for block in range(block_count)
    ]
    backs = [
        pltpu.make_async_copy(back_ref.at[slots[entry]], landed.at[entry], back_sems.at[entry])
        for entry in range(entry_count)
    ]
    outs = [
        pltpu.make_async_copy(ready.at[block], out_ref.at[pl.ds(block * rows, rows)], out_sems.at[block])
        for block in range(block_count)
    ]
    for block in range(block_count):
        for copy in [nears[block], *backs[block * fanout : (block + 1) * fanout]]:
            copy.start()
    for block in range(block_count):
        nears[block].wait()
        total = near[block]
        for entry in range(block * fanout, (block + 1) * fanout):
            backs[entry].wait()
            total = total + landed[entry].astype(F32)
        ready[block] = total.astype(BF16)
        outs[block].start()
    for copy in outs:
        copy.wait()


def cost(flops, bytes_accessed, exps):
    return pl.CostEstimate(flops=int(flops), bytes_accessed=int(bytes_accessed), transcendentals=int(exps))


def shards(token_query, token_key, token_value, cotangent, anchor_keys, anchor_values, partner, cluster, lengths):
    block_count, fanout = partner.shape
    tokens, width = token_query.shape
    rows = tokens // block_count
    anchors = anchor_keys.shape[0]
    line_size = lax.axis_size("gx")
    row_size = lax.axis_size("gy")
    entry_count = block_count * fanout
    capacity = 2 * ((entry_count // 2 + line_size - 2) // (line_size - 1))
    slot_count = line_size * capacity
    params = pltpu.CompilerParams(vmem_limit_bytes=40 * 1024 * 1024)
    large_params = pltpu.CompilerParams(vmem_limit_bytes=60 * 1024 * 1024)

    def exchange(rows_out):
        return lax.all_to_all(rows_out, "gx", split_axis=0, concat_axis=0, tiled=True)

    pair_flops = 2 * rows * rows * width
    whole = lambda *shape: pl.BlockSpec(shape, lambda step, *_: (0,) * len(shape))
    per_block = pl.BlockSpec((rows, width), lambda step, *_: (step, 0))
    block_stats = pl.BlockSpec((1, 2 * HEADS, rows), lambda step, *_: (step, 0, 0))
    turned_block = pl.BlockSpec((1, width, rows), lambda step, *_: (step, 0, 0))
    hbm = pl.BlockSpec(memory_space=pl.ANY)
    scalars = pl.BlockSpec(memory_space=pltpu.SMEM)
    stats_type = jax.ShapeDtypeStruct((block_count, 2 * HEADS, rows), F32)
    slot_stats_type = jax.ShapeDtypeStruct((slot_count, 2 * HEADS, rows), F32)
    send_type = jax.ShapeDtypeStruct((slot_count, 4 * HEADS, rows), F32)
    pair_scratch = pltpu.VMEM((PAIRS, 2 * rows, LANES), BF16)
    turned_scratch = pltpu.VMEM((PAIRS, LANES, 2 * rows), BF16)

    def slot_specs(shape):
        def spec(which):
            return pl.BlockSpec(shape, lambda step, *scalars: (scalars[-1][step * fanout + which], 0, 0))

        return [spec(which) for which in range(fanout)]

    near_stats, turned_keys, send_rows, send_slot, recv_slot = pl.pallas_call(
        functools.partial(near_stats_kernel, row_size=row_size, capacity=capacity),
        grid_spec=pltpu.PrefetchScalarGridSpec(
            num_scalar_prefetch=3,
            grid=(block_count,),
            in_specs=[
                whole(tokens, width),
                whole(tokens, width),
                whole(tokens, width),
                whole(tokens, width),
                whole(anchors, width),
                whole(anchors, width),
            ],
            out_specs=[block_stats, turned_block, hbm, scalars, scalars],
            scratch_shapes=[turned_scratch, turned_scratch, pltpu.SemaphoreType.DMA((2, entry_count))],
        ),
        out_shape=[
            stats_type,
            jax.ShapeDtypeStruct((block_count, width, rows), BF16),
            jax.ShapeDtypeStruct((slot_count, rows, 2 * width), BF16),
            jax.ShapeDtypeStruct((entry_count,), jnp.int32),
            jax.ShapeDtypeStruct((entry_count,), jnp.int32),
        ],
        compiler_params=large_params,
        cost_estimate=cost(
            2 * pair_flops * block_count * block_count * 2,
            12 * tokens * width * 2,
            HEADS * rows * rows * block_count * block_count,
        ),
        name="near_stats",
    )(
        cluster, lengths, partner.T, token_query, cotangent, token_key, token_value, anchor_keys, anchor_values
    )
    far_rows = exchange(send_rows)

    far_stats = pl.pallas_call(
        functools.partial(far_stats_kernel, fanout=fanout),
        grid_spec=pltpu.PrefetchScalarGridSpec(
            num_scalar_prefetch=1,
            grid=(block_count,),
            in_specs=[*slot_specs((1, rows, 2 * width)), per_block, per_block],
            out_specs=whole(*slot_stats_type.shape),
        ),
        out_shape=slot_stats_type,
        compiler_params=params,
        cost_estimate=cost(
            4 * pair_flops * entry_count, 4 * entry_count * rows * width * 2, HEADS * rows * rows * entry_count
        ),
        name="far_stats",
    )(recv_slot, *([far_rows] * fanout), token_key, token_value)
    got_stats = exchange(far_stats)

    totals, total_send = pl.pallas_call(
        totals_kernel,
        grid_spec=pltpu.PrefetchScalarGridSpec(
            num_scalar_prefetch=1,
            grid=(block_count,),
            in_specs=[
                whole(*stats_type.shape),
                whole(*slot_stats_type.shape),
                per_block,
                per_block,
                whole(anchors, width),
                whole(anchors, width),
            ],
            out_specs=[block_stats, whole(*send_type.shape)],
            scratch_shapes=[pltpu.VMEM((anchors, width), F32), pltpu.VMEM((anchors, width), F32)],
        ),
        out_shape=[stats_type, send_type],
        compiler_params=params,
        cost_estimate=cost(4 * pair_flops * block_count, 2 * tokens * width * 2, HEADS * anchors * tokens),
        name="totals",
    )(send_slot, near_stats, got_stats, token_query, cotangent, anchor_keys, anchor_values)
    far_totals = exchange(total_send)
    far_query = pl.pallas_call(
        functools.partial(far_query_kernel, fanout=fanout),
        grid_spec=pltpu.PrefetchScalarGridSpec(
            num_scalar_prefetch=1,
            grid=(block_count,),
            in_specs=[
                *slot_specs((1, rows, 2 * width)),
                *slot_specs((1, 2 * HEADS, rows)),
                per_block,
                per_block,
                turned_block,
            ],
            out_specs=whole(slot_count, rows, width),
        ),
        out_shape=jax.ShapeDtypeStruct((slot_count, rows, width), BF16),
        compiler_params=params,
        cost_estimate=cost(
            6 * pair_flops * entry_count, 5 * entry_count * rows * width * 2, HEADS * rows * rows * entry_count
        ),
        name="far_query",
    )(recv_slot, *([far_rows] * fanout), *([far_totals] * fanout), token_key, token_value, turned_keys)
    far_query, anchor_pieces = lax.optimization_barrier((far_query, far_totals))
    back_rows = exchange(far_query)
    anchor_share = sum_share(anchor_pieces[:, 2 * HEADS :, :])

    dquery, key_grad, value_grad = pl.pallas_call(
        functools.partial(grads_kernel, fanout=fanout),
        grid_spec=pltpu.PrefetchScalarGridSpec(
            num_scalar_prefetch=3,
            grid=(block_count,),
            in_specs=[
                per_block,
                per_block,
                whole(tokens, width),
                whole(tokens, width),
                whole(block_count, width, rows),
                whole(anchors, width),
                whole(anchors, width),
                block_stats,
                *slot_specs((1, rows, 2 * width)),
                *slot_specs((1, 2 * HEADS, rows)),
            ],
            out_specs=[per_block, whole(tokens, width), whole(tokens, width)],
            scratch_shapes=[
                pair_scratch,
                pair_scratch,
                turned_scratch,
                turned_scratch,
                pltpu.VMEM((width, anchors), BF16),
                pltpu.VMEM((PAIRS, LANES, 2 * rows), F32),
                pltpu.VMEM((tokens, width), F32),
                pltpu.VMEM((tokens, width), F32),
            ],
        ),
        out_shape=[
            jax.ShapeDtypeStruct((tokens, width), F32),
            jax.ShapeDtypeStruct((tokens, width), BF16),
            jax.ShapeDtypeStruct((tokens, width), BF16),
        ],
        compiler_params=large_params,
        cost_estimate=cost(
            10 * pair_flops * block_count * block_count,
            8 * tokens * width * 2,
            HEADS * rows * rows * block_count * block_count,
        ),
        name="near_grads",
    )(
        cluster, lengths, recv_slot, token_query, cotangent, token_key, token_value, turned_keys,
        anchor_keys, anchor_values, totals, *([far_rows] * fanout), *([far_totals] * fanout),
    )

    back_rows, anchor_share, dquery = lax.optimization_barrier((back_rows, anchor_share, dquery))
    anchor_grads = gather_anchors(anchor_share, anchors, width)
    query_grad = pl.pallas_call(
        add_kernel,
        grid_spec=pltpu.PrefetchScalarGridSpec(
            num_scalar_prefetch=1,
            grid=(1,),
            in_specs=[hbm, hbm],
            out_specs=hbm,
            scratch_shapes=[
                pltpu.VMEM((block_count, rows, width), F32),
                pltpu.VMEM((entry_count, rows, width), BF16),
                pltpu.VMEM((block_count, rows, width), BF16),
                pltpu.SemaphoreType.DMA((block_count,)),
                pltpu.SemaphoreType.DMA((entry_count,)),
                pltpu.SemaphoreType.DMA((block_count,)),
            ],
        ),
        out_shape=jax.ShapeDtypeStruct((tokens, width), BF16),
        compiler_params=large_params,
        name="add_far",
    )(send_slot, dquery, back_rows)
    return query_grad, key_grad, value_grad, anchor_grads


def sum_share(pieces):
    line_size, row_size = lax.axis_size("gx"), lax.axis_size("gy")
    share = jnp.sum(pieces.reshape(line_size, -1, *pieces.shape[1:]), axis=0)
    for step in range(row_size.bit_length() - 1):
        share = share + lax.ppermute(share, "gy", [(at, at ^ (1 << step)) for at in range(row_size)])
    return share


def gather_anchors(share, anchors, width):
    line_size = lax.axis_size("gx")
    copies = jnp.broadcast_to(share[None], (line_size, *share.shape))
    shares = lax.all_to_all(copies, "gx", split_axis=0, concat_axis=0, tiled=True)
    piece = share.shape[1] // PAIRS
    return shares.reshape(-1, PAIRS, piece, LANES).transpose(0, 2, 1, 3).reshape(2, anchors, width)


def solution(mesh):
    split = P(("gx", "gy"), None)
    return jax.shard_map(
        shards,
        mesh=mesh,
        in_specs=(split, split, split, split, P(), P(), split, split, P(("gx", "gy"))),
        out_specs=(split, split, split, P()),
        check_vma=False,
    )
```

```python
import functools

import jax
import jax.numpy as jnp
from jax import lax
from jax.experimental import pallas as pl
from jax.experimental.pallas import tpu as pltpu
from jax.sharding import PartitionSpec as P

HEADS = 8
HEAD_DIM = 64
PAIRS = HEADS // 2
LANES = 2 * HEAD_DIM
SCALE = HEAD_DIM ** (-0.5)
LOG2E = 1.4426950408889634
EXP_SCALE = SCALE * LOG2E
CHUNKS = (4, 2, 1)
F32 = jnp.float32
BF16 = jnp.bfloat16


def pair_lanes(pair):
    return slice(pair * LANES, (pair + 1) * LANES)


def dot_nt(left, right):
    return lax.dot_general(left, right, (((1,), (1,)), ((), ())), preferred_element_type=F32)


def dot_nn(left, right):
    return jnp.dot(left, right, preferred_element_type=F32)


def dot_tn(left, right):
    return lax.dot_general(left, right, (((0,), (0,)), ((), ())), preferred_element_type=F32)


def head_masks():
    lane = lax.broadcasted_iota(jnp.int32, (1, LANES), 1)
    first = jnp.where(lane < HEAD_DIM, 1.0, 0.0)
    return first.astype(BF16), (1.0 - first).astype(BF16)


def pair_rows(rows_in, masks):
    return jnp.concatenate([rows_in * masks[0], rows_in * masks[1]], axis=0)


def turned_masks(rows):
    feature = lax.broadcasted_iota(jnp.int32, (LANES, rows), 0)
    first = jnp.where(feature < HEAD_DIM, 1.0, 0.0)
    return first.astype(BF16), (1.0 - first).astype(BF16)


def turned_pair(rows_in, masks):
    turned = rows_in.T
    return jnp.concatenate([turned * masks[0], turned * masks[1]], axis=1)


def stat_row(stats, pair, offset):
    at = offset + 2 * pair
    return jnp.concatenate([stats[at : at + 1], stats[at + 1 : at + 2]], axis=1)


def store_stats(stat_ref, slot, pair, log_total, delta):
    rows = log_total.shape[1] // 2
    for at, row in ((2 * pair, log_total), (HEADS + 2 * pair, delta)):
        stat_ref[slot, at : at + 1, :] = row[:, :rows]
        stat_ref[slot, at + 1 : at + 2, :] = row[:, rows:]


def first_sums(scores, dprobs):
    highest = jnp.max(scores, axis=0, keepdims=True) * EXP_SCALE
    terms = jnp.exp2(scores * EXP_SCALE - highest)
    return highest, jnp.sum(terms, axis=0, keepdims=True), jnp.sum(terms * dprobs, axis=0, keepdims=True)


def more_sums(state, scores, dprobs):
    highest, total, mass = state
    new_highest = jnp.maximum(highest, jnp.max(scores, axis=0, keepdims=True) * EXP_SCALE)
    shrink = jnp.exp2(highest - new_highest)
    terms = jnp.exp2(scores * EXP_SCALE - new_highest)
    return (
        new_highest,
        total * shrink + jnp.sum(terms, axis=0, keepdims=True),
        mass * shrink + jnp.sum(terms * dprobs, axis=0, keepdims=True),
    )


def finish_sums(state):
    highest, total, mass = state
    return highest + jnp.log(total) * LOG2E, mass / total


def weights_of(scores, dprobs, log_total, delta):
    weights = jnp.exp2(scores * EXP_SCALE - log_total)
    return weights.astype(BF16), (weights * (dprobs - delta)).astype(BF16)


def together(parts, axis):
    return parts[0] if len(parts) == 1 else jnp.concatenate(parts, axis=axis)


def staggered(items, begin, finish):
    ahead = None
    for item in items:
        begun = begin(item)
        if ahead is not None:
            finish(*ahead)
        ahead = (item, begun)
    finish(*ahead)


def block_rows_at(index, rows):
    return pl.ds(pl.multiple_of(index * rows, rows), rows)


def in_chunks(count, work, state):
    done = 0
    for size in CHUNKS:
        until = count // size
        state = lax.fori_loop(done // size, until, lambda at, held, size=size: work(at * size, size, held), state)
        done = until * size
    return state


def entry_slots(partner, block_count, row_size, capacity):
    fanout = partner.shape[0]
    entry_count = block_count * fanout
    targets = [partner[entry % fanout, entry // fanout] for entry in range(entry_count)]
    peers = [target // (block_count * row_size) for target in targets]
    order = [target * fanout + entry % fanout for entry, target in enumerate(targets)]
    sent_before, got_before = [0] * entry_count, [0] * entry_count
    for left in range(entry_count):
        for right in range(left + 1, entry_count):
            same = (peers[left] == peers[right]).astype(jnp.int32)
            swapped = jnp.where(order[right] < order[left], same, 0)
            sent_before[left] = sent_before[left] + swapped
            sent_before[right] = sent_before[right] + (same - swapped)
            got_before[right] = got_before[right] + same
    firsts = [peer * capacity for peer in peers]
    sent = [first + count for first, count in zip(firsts, sent_before)]
    return sent, [first + count for first, count in zip(firsts, got_before)]


def near_stats_kernel(
    cluster, lengths, partner, query_ref, cotan_ref, key_ref, value_ref, akey_ref, avalue_ref,
    stat_ref, keyt_ref, send_ref, send_slot, recv_slot, qturn, oturn, sems, *, row_size, capacity,
):
    block = pl.program_id(0)
    block_count = pl.num_programs(0)
    rows, width = stat_ref.shape[2], query_ref.shape[1]
    fanout = partner.shape[0]

    def send_copies(slots):
        for entry, slot in enumerate(slots):
            own = pl.ds(entry // fanout * rows, rows)
            into = send_ref.at[slot]
            yield pltpu.make_async_copy(query_ref.at[own], into.at[:, pl.ds(0, width)], sems.at[0, entry])
            yield pltpu.make_async_copy(cotan_ref.at[own], into.at[:, pl.ds(width, width)], sems.at[1, entry])

    @pl.when(block == 0)
    def _():
        sent, received = entry_slots(partner, block_count_of(query_ref, rows), row_size, capacity)
        for copy in send_copies(sent):
            copy.start()
        for entry in range(len(sent)):
            send_slot[entry] = sent[entry]
            recv_slot[entry] = received[entry]

    masks = turned_masks(rows)
    own = block_rows_at(block, rows)
    first_at = block_rows_at(cluster[block, 0], rows)
    start = [None] * PAIRS

    def begin_first(pair):
        lanes = pair_lanes(pair)
        queries = turned_pair(query_ref[own, lanes], masks)
        cotans = turned_pair(cotan_ref[own, lanes], masks)
        qturn[pair] = queries
        oturn[pair] = cotans
        keyt_ref[0, lanes, :] = key_ref[own, lanes].T
        keys = together([akey_ref[:, lanes], key_ref[first_at, lanes]], 0)
        values = together([avalue_ref[:, lanes], value_ref[first_at, lanes]], 0)
        return dot_nn(keys, queries), dot_nn(values, cotans)

    def finish_first(pair, tiles):
        start[pair] = first_sums(*tiles)

    staggered(range(PAIRS), begin_first, finish_first)

    def work(first, count, states):
        spots = [
            block_rows_at(cluster[block, 1 + first + which], rows) for which in range(count)
        ]
        states = list(states)

        def begin(pair):
            lanes = pair_lanes(pair)
            return (
                dot_nn(together([key_ref[at, lanes] for at in spots], 0), qturn[pair]),
                dot_nn(together([value_ref[at, lanes] for at in spots], 0), oturn[pair]),
            )

        def finish(pair, tiles):
            states[pair] = more_sums(states[pair], *tiles)

        staggered(range(PAIRS), begin, finish)
        return tuple(states)

    states = in_chunks(lengths[block] - 1, work, tuple(start))
    for pair in range(PAIRS):
        store_stats(stat_ref, 0, pair, *finish_sums(states[pair]))

    @pl.when(block == block_count - 1)
    def _():
        for copy in send_copies([0] * (block_count_of(query_ref, rows) * fanout)):
            copy.wait()


def block_count_of(rows_ref, rows):
    return rows_ref.shape[0] // rows


def far_tiles(far_ref, keys, values, pair, masks):
    lanes = pair_lanes(pair)
    width = far_ref.shape[2] // 2
    queries = pair_rows(far_ref[0, :, lanes], masks)
    cotans = pair_rows(far_ref[0, :, width + lanes.start : width + lanes.stop], masks)
    return dot_nt(keys, queries), dot_nt(values, cotans), queries, cotans


def far_stats_kernel(slots, *refs, fanout):
    far_refs, (key_ref, value_ref, stat_ref) = refs[:fanout], refs[fanout:]
    masks = head_masks()
    step = pl.program_id(0)

    def begin(item):
        which, pair = item
        return far_tiles(far_refs[which], key_ref[:, pair_lanes(pair)], value_ref[:, pair_lanes(pair)], pair, masks)

    def finish(item, tiles):
        which, pair = item
        store_stats(stat_ref, slots[step * fanout + which], pair, *finish_sums(first_sums(*tiles[:2])))

    staggered([(which, pair) for which in range(fanout) for pair in range(PAIRS)], begin, finish)


def totals_kernel(
    slots, near_ref, far_ref, query_ref, cotan_ref, akey_ref, avalue_ref, total_ref, send_ref, key_acc, value_acc
):
    block = pl.program_id(0)
    block_count = pl.num_programs(0)
    fanout = slots.shape[0] // near_ref.shape[0]

    @pl.when(block == 0)
    def _():
        key_acc[...] = jnp.zeros_like(key_acc)
        value_acc[...] = jnp.zeros_like(value_acc)

    mine = [slots[block * fanout + which] for which in range(fanout)]
    parts = [near_ref[block]] + [far_ref[slot] for slot in mine]
    logs = [part[:HEADS] for part in parts]
    highest = functools.reduce(jnp.maximum, logs)
    shares = [jnp.exp2(log - highest) for log in logs]
    total = sum(shares)
    mass = sum(share * part[HEADS:] for share, part in zip(shares, parts))
    stats = jnp.concatenate([highest + jnp.log(total) * LOG2E, mass / total], axis=0)
    total_ref[0] = stats
    for slot in mine:
        send_ref[slot, : 2 * HEADS, :] = stats

    masks = head_masks()

    def begin(pair):
        lanes = pair_lanes(pair)
        qpair = pair_rows(query_ref[:, lanes], masks)
        opair = pair_rows(cotan_ref[:, lanes], masks)
        return dot_nt(akey_ref[:, lanes], qpair), dot_nt(avalue_ref[:, lanes], opair), qpair, opair

    def finish(pair, tiles):
        scores, dprobs, qpair, opair = tiles
        weights, dscore = weights_of(scores, dprobs, stat_row(stats, pair, 0), stat_row(stats, pair, HEADS))
        key_acc[:, pair_lanes(pair)] += dot_nn(dscore, qpair)
        value_acc[:, pair_lanes(pair)] += dot_nn(weights, opair)

    staggered(range(PAIRS), begin, finish)

    @pl.when(block == block_count - 1)
    def _():
        slot_count = send_ref.shape[0]
        piece = 2 * key_acc.shape[0] // slot_count
        for slot in range(slot_count):
            acc, factor = (key_acc, SCALE) if slot < slot_count // 2 else (value_acc, 1.0)
            first = slot % (slot_count // 2) * piece
            for pair in range(PAIRS):
                at = 2 * HEADS + pair * piece
                send_ref[slot, at : at + piece, :] = acc[first : first + piece, pair_lanes(pair)] * factor


def unpair_turned(both):
    rows = both.shape[1] // 2
    feature = lax.broadcasted_iota(jnp.int32, (LANES, rows), 0)
    return jnp.where(feature < HEAD_DIM, both[:, :rows], both[:, rows:]).T


def far_query_kernel(slots, *refs, fanout):
    far_refs, stat_refs, refs = refs[:fanout], refs[fanout : 2 * fanout], refs[2 * fanout :]
    key_ref, value_ref, keyt_ref, out_ref = refs
    masks = head_masks()
    step = pl.program_id(0)
    stats = [stat_ref[0] for stat_ref in stat_refs]

    def begin(item):
        which, pair = item
        return far_tiles(far_refs[which], key_ref[:, pair_lanes(pair)], value_ref[:, pair_lanes(pair)], pair, masks)

    def finish(item, tiles):
        which, pair = item
        logs, deltas = stat_row(stats[which], pair, 0), stat_row(stats[which], pair, HEADS)
        _, dscore = weights_of(*tiles[:2], logs, deltas)
        far_grad = unpair_turned(dot_nn(keyt_ref[0, pair_lanes(pair), :], dscore)) * SCALE
        out_ref[slots[step * fanout + which], :, pair_lanes(pair)] = far_grad.astype(BF16)

    staggered([(which, pair) for which in range(fanout) for pair in range(PAIRS)], begin, finish)


def grads_kernel(
    cluster, lengths, slots, query_ref, cotan_ref, key_ref, value_ref, keyt_ref, akey_ref, avalue_ref, total_ref,
    *refs, fanout,
):
    far_refs, stat_refs, refs = refs[:fanout], refs[fanout : 2 * fanout], refs[2 * fanout :]
    dquery_ref, dkey_ref, dvalue_ref, qpair, opair, qturn, oturn, aturn, dq_acc, dk_acc, dv_acc = refs
    block = pl.program_id(0)
    block_count = pl.num_programs(0)
    rows, width = query_ref.shape

    @pl.when(block == 0)
    def _():
        dk_acc[...] = jnp.zeros_like(dk_acc)
        dv_acc[...] = jnp.zeros_like(dv_acc)
        for pair in range(PAIRS):
            aturn[pair_lanes(pair), :] = akey_ref[:, pair_lanes(pair)].T

    masks = head_masks()
    lane_masks = turned_masks(rows)
    stats = total_ref[0]
    logs = [stat_row(stats, pair, 0) for pair in range(PAIRS)]
    deltas = [stat_row(stats, pair, HEADS) for pair in range(PAIRS)]

    first_id = cluster[block, 0]
    first_at = block_rows_at(first_id, rows)

    def begin_first(pair):
        lanes = pair_lanes(pair)
        queries = turned_pair(query_ref[:, lanes], lane_masks)
        cotans = turned_pair(cotan_ref[:, lanes], lane_masks)
        qturn[pair] = queries
        oturn[pair] = cotans
        qpair[pair] = pair_rows(query_ref[:, lanes], masks)
        opair[pair] = pair_rows(cotan_ref[:, lanes], masks)
        keys = together([key_ref[first_at, lanes], akey_ref[:, lanes]], 0)
        values = together([value_ref[first_at, lanes], avalue_ref[:, lanes]], 0)
        return dot_nn(keys, queries), dot_nn(values, cotans)

    def finish_first(pair, tiles):
        lanes = pair_lanes(pair)
        weights, dscore = weights_of(*tiles, logs[pair], deltas[pair])
        dk_acc[first_at, lanes] += dot_nn(dscore[:rows], qpair[pair])
        dv_acc[first_at, lanes] += dot_nn(weights[:rows], opair[pair])
        dq_acc[pair] = dot_nn(together([keyt_ref[first_id, lanes, :], aturn[lanes, :]], 1), dscore)

    staggered(range(PAIRS), begin_first, finish_first)

    def work(first, count, carry):
        ids = [cluster[block, 1 + first + which] for which in range(count)]
        spots = [block_rows_at(index, rows) for index in ids]

        def begin(pair):
            lanes = pair_lanes(pair)
            return (
                dot_nn(together([key_ref[at, lanes] for at in spots], 0), qturn[pair]),
                dot_nn(together([value_ref[at, lanes] for at in spots], 0), oturn[pair]),
            )

        def finish(pair, tiles):
            lanes = pair_lanes(pair)
            weights, dscore = weights_of(*tiles, logs[pair], deltas[pair])
            key_part = dot_nn(dscore, qpair[pair])
            value_part = dot_nn(weights, opair[pair])
            for which, at in enumerate(spots):
                part = slice(which * rows, (which + 1) * rows)
                dk_acc[at, lanes] += key_part[part]
                dv_acc[at, lanes] += value_part[part]
            dq_acc[pair] += dot_nn(together([keyt_ref[index, lanes, :] for index in ids], 1), dscore)

        staggered(range(PAIRS), begin, finish)
        return carry

    in_chunks(lengths[block] - 1, work, 0)
    for pair in range(PAIRS):
        dquery_ref[:, pair_lanes(pair)] = unpair_turned(dq_acc[pair]) * SCALE

    own = block_rows_at(block, rows)
    far_stats = [stat_ref[0] for stat_ref in stat_refs]

    def begin_far(pair):
        keys, values = key_ref[own, pair_lanes(pair)], value_ref[own, pair_lanes(pair)]
        return [far_tiles(far_ref, keys, values, pair, masks) for far_ref in far_refs]

    def finish_far(pair, tiles):
        lanes = pair_lanes(pair)
        both = [
            weights_of(*tile[:2], stat_row(far_stat, pair, 0), stat_row(far_stat, pair, HEADS))
            for tile, far_stat in zip(tiles, far_stats)
        ]
        dscores, weights = [dscore for _, dscore in both], [weights for weights, _ in both]
        dk_acc[own, lanes] += dot_nn(together(dscores, 1), together([tile[2] for tile in tiles], 0))
        dv_acc[own, lanes] += dot_nn(together(weights, 1), together([tile[3] for tile in tiles], 0))

    staggered(range(PAIRS), begin_far, finish_far)

    @pl.when(block == block_count - 1)
    def _():
        dkey_ref[...] = (dk_acc[...] * SCALE).astype(BF16)
        dvalue_ref[...] = dv_acc[...].astype(BF16)


def add_kernel(slots, near_ref, back_ref, out_ref, near, landed, ready, near_sems, back_sems, out_sems):
    entry_count, rows = landed.shape[:2]
    block_count = near.shape[0]
    fanout = entry_count // block_count
    nears = [
        pltpu.make_async_copy(near_ref.at[pl.ds(block * rows, rows)], near.at[block], near_sems.at[block])
        for block in range(block_count)
    ]
    backs = [
        pltpu.make_async_copy(back_ref.at[slots[entry]], landed.at[entry], back_sems.at[entry])
        for entry in range(entry_count)
    ]
    outs = [
        pltpu.make_async_copy(ready.at[block], out_ref.at[pl.ds(block * rows, rows)], out_sems.at[block])
        for block in range(block_count)
    ]
    for block in range(block_count):
        for copy in [nears[block], *backs[block * fanout : (block + 1) * fanout]]:
            copy.start()
    for block in range(block_count):
        nears[block].wait()
        total = near[block]
        for entry in range(block * fanout, (block + 1) * fanout):
            backs[entry].wait()
            total = total + landed[entry].astype(F32)
        ready[block] = total.astype(BF16)
        outs[block].start()
    for copy in outs:
        copy.wait()


def cost(flops, bytes_accessed, exps):
    return pl.CostEstimate(flops=int(flops), bytes_accessed=int(bytes_accessed), transcendentals=int(exps))


def shards(token_query, token_key, token_value, cotangent, anchor_keys, anchor_values, partner, cluster, lengths):
    block_count, fanout = partner.shape
    tokens, width = token_query.shape
    rows = tokens // block_count
    anchors = anchor_keys.shape[0]
    line_size = lax.axis_size("gx")
    row_size = lax.axis_size("gy")
    entry_count = block_count * fanout
    capacity = 2 * ((entry_count // 2 + line_size - 2) // (line_size - 1))
    slot_count = line_size * capacity
    params = pltpu.CompilerParams(vmem_limit_bytes=40 * 1024 * 1024)
    large_params = pltpu.CompilerParams(vmem_limit_bytes=60 * 1024 * 1024)

    def exchange(rows_out):
        return lax.all_to_all(rows_out, "gx", split_axis=0, concat_axis=0, tiled=True)

    pair_flops = 2 * rows * rows * width
    whole = lambda *shape: pl.BlockSpec(shape, lambda step, *_: (0,) * len(shape))
    per_block = pl.BlockSpec((rows, width), lambda step, *_: (step, 0))
    block_stats = pl.BlockSpec((1, 2 * HEADS, rows), lambda step, *_: (step, 0, 0))
    turned_block = pl.BlockSpec((1, width, rows), lambda step, *_: (step, 0, 0))
    hbm = pl.BlockSpec(memory_space=pl.ANY)
    scalars = pl.BlockSpec(memory_space=pltpu.SMEM)
    stats_type = jax.ShapeDtypeStruct((block_count, 2 * HEADS, rows), F32)
    slot_stats_type = jax.ShapeDtypeStruct((slot_count, 2 * HEADS, rows), F32)
    send_type = jax.ShapeDtypeStruct((slot_count, 4 * HEADS, rows), F32)
    pair_scratch = pltpu.VMEM((PAIRS, 2 * rows, LANES), BF16)
    turned_scratch = pltpu.VMEM((PAIRS, LANES, 2 * rows), BF16)

    def slot_specs(shape):
        def spec(which):
            return pl.BlockSpec(shape, lambda step, *scalars: (scalars[-1][step * fanout + which], 0, 0))

        return [spec(which) for which in range(fanout)]

    near_stats, turned_keys, send_rows, send_slot, recv_slot = pl.pallas_call(
        functools.partial(near_stats_kernel, row_size=row_size, capacity=capacity),
        grid_spec=pltpu.PrefetchScalarGridSpec(
            num_scalar_prefetch=3,
            grid=(block_count,),
            in_specs=[
                whole(tokens, width),
                whole(tokens, width),
                whole(tokens, width),
                whole(tokens, width),
                whole(anchors, width),
                whole(anchors, width),
            ],
            out_specs=[block_stats, turned_block, hbm, scalars, scalars],
            scratch_shapes=[turned_scratch, turned_scratch, pltpu.SemaphoreType.DMA((2, entry_count))],
        ),
        out_shape=[
            stats_type,
            jax.ShapeDtypeStruct((block_count, width, rows), BF16),
            jax.ShapeDtypeStruct((slot_count, rows, 2 * width), BF16),
            jax.ShapeDtypeStruct((entry_count,), jnp.int32),
            jax.ShapeDtypeStruct((entry_count,), jnp.int32),
        ],
        compiler_params=large_params,
        cost_estimate=cost(
            2 * pair_flops * block_count * block_count * 2,
            12 * tokens * width * 2,
            HEADS * rows * rows * block_count * block_count,
        ),
        name="near_stats",
    )(
        cluster, lengths, partner.T, token_query, cotangent, token_key, token_value, anchor_keys, anchor_values
    )
    far_rows = exchange(send_rows)

    far_stats = pl.pallas_call(
        functools.partial(far_stats_kernel, fanout=fanout),
        grid_spec=pltpu.PrefetchScalarGridSpec(
            num_scalar_prefetch=1,
            grid=(block_count,),
            in_specs=[*slot_specs((1, rows, 2 * width)), per_block, per_block],
            out_specs=whole(*slot_stats_type.shape),
        ),
        out_shape=slot_stats_type,
        compiler_params=params,
        cost_estimate=cost(
            4 * pair_flops * entry_count, 4 * entry_count * rows * width * 2, HEADS * rows * rows * entry_count
        ),
        name="far_stats",
    )(recv_slot, *([far_rows] * fanout), token_key, token_value)
    got_stats = exchange(far_stats)

    totals, total_send = pl.pallas_call(
        totals_kernel,
        grid_spec=pltpu.PrefetchScalarGridSpec(
            num_scalar_prefetch=1,
            grid=(block_count,),
            in_specs=[
                whole(*stats_type.shape),
                whole(*slot_stats_type.shape),
                per_block,
                per_block,
                whole(anchors, width),
                whole(anchors, width),
            ],
            out_specs=[block_stats, whole(*send_type.shape)],
            scratch_shapes=[pltpu.VMEM((anchors, width), F32), pltpu.VMEM((anchors, width), F32)],
        ),
        out_shape=[stats_type, send_type],
        compiler_params=params,
        cost_estimate=cost(4 * pair_flops * block_count, 2 * tokens * width * 2, HEADS * anchors * tokens),
        name="totals",
    )(send_slot, near_stats, got_stats, token_query, cotangent, anchor_keys, anchor_values)
    far_totals = exchange(total_send)
    far_query = pl.pallas_call(
        functools.partial(far_query_kernel, fanout=fanout),
        grid_spec=pltpu.PrefetchScalarGridSpec(
            num_scalar_prefetch=1,
            grid=(block_count,),
            in_specs=[
                *slot_specs((1, rows, 2 * width)),
                *slot_specs((1, 2 * HEADS, rows)),
                per_block,
                per_block,
                turned_block,
            ],
            out_specs=whole(slot_count, rows, width),
        ),
        out_shape=jax.ShapeDtypeStruct((slot_count, rows, width), BF16),
        compiler_params=params,
        cost_estimate=cost(
            6 * pair_flops * entry_count, 5 * entry_count * rows * width * 2, HEADS * rows * rows * entry_count
        ),
        name="far_query",
    )(recv_slot, *([far_rows] * fanout), *([far_totals] * fanout), token_key, token_value, turned_keys)
    far_query, anchor_pieces = lax.optimization_barrier((far_query, far_totals))
    back_rows = exchange(far_query)
    anchor_share = sum_share(anchor_pieces[:, 2 * HEADS :, :])

    dquery, key_grad, value_grad = pl.pallas_call(
        functools.partial(grads_kernel, fanout=fanout),
        grid_spec=pltpu.PrefetchScalarGridSpec(
            num_scalar_prefetch=3,
            grid=(block_count,),
            in_specs=[
                per_block,
                per_block,
                whole(tokens, width),
                whole(tokens, width),
                whole(block_count, width, rows),
                whole(anchors, width),
                whole(anchors, width),
                block_stats,
                *slot_specs((1, rows, 2 * width)),
                *slot_specs((1, 2 * HEADS, rows)),
            ],
            out_specs=[per_block, whole(tokens, width), whole(tokens, width)],
            scratch_shapes=[
                pair_scratch,
                pair_scratch,
                turned_scratch,
                turned_scratch,
                pltpu.VMEM((width, anchors), BF16),
                pltpu.VMEM((PAIRS, LANES, 2 * rows), F32),
                pltpu.VMEM((tokens, width), F32),
                pltpu.VMEM((tokens, width), F32),
            ],
        ),
        out_shape=[
            jax.ShapeDtypeStruct((tokens, width), F32),
            jax.ShapeDtypeStruct((tokens, width), BF16),
            jax.ShapeDtypeStruct((tokens, width), BF16),
        ],
        compiler_params=large_params,
        cost_estimate=cost(
            10 * pair_flops * block_count * block_count,
            8 * tokens * width * 2,
            HEADS * rows * rows * block_count * block_count,
        ),
        name="near_grads",
    )(
        cluster, lengths, recv_slot, token_query, cotangent, token_key, token_value, turned_keys,
        anchor_keys, anchor_values, totals, *([far_rows] * fanout), *([far_totals] * fanout),
    )

    back_rows, anchor_share, dquery = lax.optimization_barrier((back_rows, anchor_share, dquery))
    anchor_grads = gather_anchors(anchor_share, anchors, width)
    query_grad = pl.pallas_call(
        add_kernel,
        grid_spec=pltpu.PrefetchScalarGridSpec(
            num_scalar_prefetch=1,
            grid=(1,),
            in_specs=[hbm, hbm],
            out_specs=hbm,
            scratch_shapes=[
                pltpu.VMEM((block_count, rows, width), F32),
                pltpu.VMEM((entry_count, rows, width), BF16),
                pltpu.VMEM((block_count, rows, width), BF16),
                pltpu.SemaphoreType.DMA((block_count,)),
                pltpu.SemaphoreType.DMA((entry_count,)),
                pltpu.SemaphoreType.DMA((block_count,)),
            ],
        ),
        out_shape=jax.ShapeDtypeStruct((tokens, width), BF16),
        compiler_params=large_params,
        name="add_far",
    )(send_slot, dquery, back_rows)
    return query_grad, key_grad, value_grad, anchor_grads


def sum_share(pieces):
    line_size, row_size = lax.axis_size("gx"), lax.axis_size("gy")
    share = jnp.sum(pieces.reshape(line_size, -1, *pieces.shape[1:]), axis=0)
    for step in range(row_size.bit_length() - 1):
        share = share + lax.ppermute(share, "gy", [(at, at ^ (1 << step)) for at in range(row_size)])
    return share


def gather_anchors(share, anchors, width):
    line_size = lax.axis_size("gx")
    copies = jnp.broadcast_to(share[None], (line_size, *share.shape))
    shares = lax.all_to_all(copies, "gx", split_axis=0, concat_axis=0, tiled=True)
    piece = share.shape[1] // PAIRS
    return shares.reshape(-1, PAIRS, piece, LANES).transpose(0, 2, 1, 3).reshape(2, anchors, width)


def solution(mesh):
    split = P(("gx", "gy"), None)
    return jax.shard_map(
        shards,
        mesh=mesh,
        in_specs=(split, split, split, split, P(), P(), split, split, P(("gx", "gy"))),
        out_specs=(split, split, split, P()),
        check_vma=False,
    )
```
